128 devices in a mesh: gx: 16 (over z, x), gy: 8 (over y, core).
Axes of the slice: x: 4, y: 4, z: 4, core: 2. Of those that a mesh axis runs over, the one named last changes fastest.
Arguments:
- background: bfloat16 [16384, 8, 512], P(('gx', 'gy')), may hold values from -6 to 6
- col_target: int32 [16384], P(('gx', 'gy')), may hold values from 0 to 255, as said below
- obs_pert: bfloat16 [16384, 512], P(('gx', 'gy')), may hold values from -64 to 64
- innovation: float32 [16384], P(('gx', 'gy')), may hold values from -6 to 6
- obs_rinv: float32 [16384], P(('gx', 'gy')), may hold values from 0.1 to 1
- obs_loc: float32 [2, 16384], P(None, ('gx', 'gy')), may hold values from 0.2 to 1
- obs_patch: int32 [2, 16384], P(None, ('gx', 'gy')), may hold values from 0 to 255, as said below
Outputs:
- analysed: bfloat16 [16384, 8, 512], P(('gx', 'gy'))
The draws below stay inside these ranges and needn't reach their ends.
Inputs may be any that keep to these rules, and one draw needn't show every extreme that they name: Column c belongs to patch col_target[c], owned by device col_target[c] // 2; patches are dealt to owners to balance observation load, not by geography. Among the 128 columns of one device at most 2 belong to patches of one owner; in every draw one owner gets exactly 2 columns from every device. `obs_patch`: the 2 entries of an observation name different patches. Among the 256 entries of one device at most 4 name patches of one owner; in every draw one owner is named exactly 4 times by every device.
All inputs are finite; a program needn't handle non-finite values. Where the reference program divides by a largest or mean magnitude, that divisor is 1e-20 or more.
Results may differ from the reference program's by a relative error of at most 0.0057.
Values may be sent and summed in bfloat16 or wider, within the bound.
No kernel may reach another device: no remote copies, remote signals or barrier semaphores. Data moves between devices by JAX's collectives and lax.ppermute only.
A program may use at most 64 MiB of HBM per device.

```python
import math
import jax
import jax.numpy as jnp
from jax import lax

K = 512
LEV = 8
COLS_DEV = 128
OBS_DEV = 128
PATCH_DEV = 2
REACH = 2
STEPS = 4
COLUMNS = 16384
OBS = 16384
PATCHES = 256
CAP = 2
OCAP = 4


def owner_lists(key, per_device, slot_cap):
    num_owners = PATCHES // PATCH_DEV
    busiest = jax.random.randint(jax.random.fold_in(key, 1), (), 0, num_owners)

    def one_device(device_key):
        key_spare, key_offset, key_order = jax.random.split(device_key, 3)
        spare_slots = jax.random.permutation(key_spare, num_owners * slot_cap - slot_cap).astype(jnp.int32) + slot_cap
        chosen = jnp.concatenate([jnp.arange(slot_cap, dtype=jnp.int32), spare_slots[:per_device - slot_cap]])
        offsets = jnp.concatenate([jnp.zeros((1,), jnp.int32), jax.random.permutation(key_offset, num_owners - 1).astype(jnp.int32) + 1])
        owner_ids = (busiest + offsets[chosen // slot_cap]) % num_owners
        return jax.random.permutation(key_order, owner_ids)
    device_keys = jax.random.split(jax.random.fold_in(key, 2), num_owners)
    return jax.vmap(one_device)(device_keys).astype(jnp.int32)


def draw_col_target(key, part):
    key = jax.random.fold_in(key, 3)
    owner_ids = owner_lists(key, COLS_DEV, CAP).reshape(-1)
    local_patch = jax.random.randint(jax.random.fold_in(key, 4), owner_ids.shape, 0, PATCH_DEV)
    return (owner_ids * PATCH_DEV + local_patch).astype(jnp.int32)


def draw_obs_patch(key, part):
    key = jax.random.fold_in(key, 5)
    owner_ids = owner_lists(key, REACH * OBS_DEV, OCAP).reshape(-1, REACH, OBS_DEV)
    flip_bits = jax.random.randint(jax.random.fold_in(key, 6), (owner_ids.shape[0], 1, OBS_DEV), 0, PATCH_DEV)
    local_patch = (jnp.arange(REACH, dtype=jnp.int32)[None, :, None] + flip_bits) % PATCH_DEV
    patch_ids = owner_ids * PATCH_DEV + local_patch
    return jnp.transpose(patch_ids, (1, 0, 2)).reshape(REACH, OBS).astype(jnp.int32)


def draw_obs_pert(key, part):
    key = jax.random.fold_in(key, 7)
    key_member, key_core = jax.random.split(key, 2)
    member_scale = jnp.exp(jax.random.uniform(key_member, (1, K), jnp.float32, math.log(0.5), math.log(5.0)))
    values = jnp.clip(jax.random.normal(key_core, (OBS, K), jnp.float32), -4.0, 4.0) * member_scale
    return values.astype(jnp.bfloat16)


def shard_levels(rng, extent, cuts, low, top_value):
    level = 1.0
    for position, parts in cuts:
        draws = jax.random.uniform(jax.random.fold_in(jax.random.fold_in(rng, 6), position), (parts,), jnp.float32, low / len(cuts), top_value / len(cuts))
        level = level * jnp.repeat(jnp.exp(draws), extent[position] // parts).reshape((-1,) + (1,) * (len(extent) - 1 - position))
    return level


def noise(key, extent, deviation, bound, cuts=(), held_as=jnp.bfloat16):
    drawn = deviation * jax.random.normal(key, extent, jnp.float32)
    if cuts:
        drawn = drawn * shard_levels(key, extent, cuts, -0.22, 0.18)
    return jnp.clip(drawn, -bound, bound).astype(held_as)


def setup_inputs(seed: int = 0) -> dict:
    keys = jax.random.split(jax.random.key(seed), 8)
    return {
        "background": noise(keys[0], (COLUMNS, LEV, K), 1.0, 6.0, ((0, 128),)),
        "col_target": draw_col_target(jax.random.fold_in(keys[7], 71), 0),
        "obs_pert": draw_obs_pert(jax.random.fold_in(keys[7], 71), 0),
        "innovation": noise(keys[3], (OBS,), 1.0, 6.0, ((0, 128),), jnp.float32),
        "obs_rinv": jnp.clip(jnp.exp(math.log(1.0) - 2.3025851 * jax.random.uniform(keys[4], (OBS,), jnp.float32) ** shard_levels(keys[4], (OBS,), ((0, 128),), -0.2, 0.2)), 0.1, 1.0),
        "obs_loc": jnp.clip(0.2 + 0.8 * jax.random.uniform(keys[5], (REACH, OBS), jnp.float32) ** shard_levels(keys[5], (REACH, OBS), ((1, 128),), -0.2, 0.2), 0.2, 1.0),
        "obs_patch": draw_obs_patch(jax.random.fold_in(keys[7], 71), 0),
    }


def square_root(system):
    members = system.shape[0]
    identity = jnp.eye(members, dtype=system.dtype)
    bound_sum = jnp.max(lax.optimization_barrier(jnp.sum(jnp.abs(system), axis=1)))
    current = system / bound_sum
    inverse = identity
    for _ in range(STEPS):
        middle = 1.5 * identity - 0.5 * jnp.dot(inverse, current, precision=lax.Precision.HIGHEST)
        current = jnp.dot(current, middle, precision=lax.Precision.HIGHEST)
        inverse = jnp.dot(middle, inverse, precision=lax.Precision.HIGHEST)
    return (inverse, bound_sum)

def patch_weights(weighted_rows, scaled_innov, patch_tags, patch):
    chosen = patch_tags == patch
    masked = jnp.where(chosen[:, None], weighted_rows, jnp.zeros_like(weighted_rows))
    gram_matrix = lax.dot_general(masked, masked, (((0,), (0,)), ((), ())), preferred_element_type=jnp.float32)
    lifted = jnp.where(chosen, scaled_innov.astype(jnp.float32), jnp.zeros((), jnp.float32))
    obs_pull = jnp.dot(lifted, masked.astype(jnp.float32), precision=lax.Precision.HIGHEST)
    members = weighted_rows.shape[1]
    system = gram_matrix + (members - 1) * jnp.eye(members, dtype=gram_matrix.dtype)
    inverse, bound_sum = square_root(system)
    analysis_cov = jnp.dot(inverse, inverse, precision=lax.Precision.HIGHEST) / bound_sum
    mean_weight = jnp.dot(analysis_cov, obs_pull, precision=lax.Precision.HIGHEST)
    return (jnp.sqrt((members - 1) / bound_sum) * inverse + mean_weight[:, None]).astype(jnp.bfloat16)

def owner_order(owner_ids, num_owners, slot_total, filler):
    order = jnp.argsort(owner_ids, stable=True).astype(jnp.int32)
    sizes = jax.ops.segment_sum(jnp.ones_like(owner_ids), owner_ids, num_segments=num_owners).astype(jnp.int32)
    starts = (jnp.cumsum(sizes) - sizes).astype(jnp.int32)
    padded = jnp.concatenate([order, jnp.full((slot_total,), filler, jnp.int32)])
    return (padded, starts, sizes)

def reference(background, col_target, obs_pert, innovation, obs_rinv, obs_loc, obs_patch):
    num_owners = PATCHES // PATCH_DEV
    members = background.shape[2]
    col_slots = num_owners * CAP
    pair_slots = num_owners * OCAP
    pair_total = REACH * OBS
    col_order, col_starts, col_sizes = owner_order(col_target // PATCH_DEV, num_owners, col_slots, COLUMNS)
    pair_patch = obs_patch.reshape(-1)
    pair_obs = jnp.tile(jnp.arange(OBS, dtype=jnp.int32), REACH)
    pair_weight = jnp.tile(obs_rinv, REACH) * obs_loc.reshape(-1)
    pair_order, pair_starts, pair_sizes = owner_order(pair_patch // PATCH_DEV, num_owners, pair_slots, pair_total)

    def visit_owner(result, owner_index):
        col_index = lax.dynamic_slice(col_order, (col_starts[owner_index],), (col_slots,))
        col_valid = jnp.arange(col_slots, dtype=jnp.int32) < col_sizes[owner_index]
        col_safe = jnp.minimum(col_index, COLUMNS - 1)
        columns = background[col_safe]
        col_tags = jnp.where(col_valid, col_target[col_safe] % PATCH_DEV, -1)
        pair_index = lax.dynamic_slice(pair_order, (pair_starts[owner_index],), (pair_slots,))
        pair_valid = jnp.arange(pair_slots, dtype=jnp.int32) < pair_sizes[owner_index]
        pair_safe = jnp.minimum(pair_index, pair_total - 1)
        obs_index = pair_obs[pair_safe]
        root_weight = jnp.where(pair_valid, jnp.sqrt(pair_weight[pair_safe]), jnp.zeros((), pair_weight.dtype))
        weighted_rows = (root_weight[:, None] * obs_pert[obs_index].astype(jnp.float32)).astype(jnp.bfloat16)
        scaled_innov = (root_weight * innovation[obs_index]).astype(jnp.bfloat16)
        pair_tags = jnp.where(pair_valid, pair_patch[pair_safe] % PATCH_DEV, -1)
        widened = columns.astype(jnp.float32)
        member_mean = lax.optimization_barrier(jnp.mean(widened, axis=-1, keepdims=True))
        spread = (widened - member_mean).astype(jnp.bfloat16).reshape(-1, members)
        analysed = jnp.zeros_like(columns)
        for patch in range(PATCH_DEV):
            weights = patch_weights(weighted_rows, scaled_innov, pair_tags, patch)
            increment = jnp.dot(spread, weights, preferred_element_type=jnp.float32).reshape(columns.shape)
            analysed = jnp.where((col_tags == patch)[:, None, None], (member_mean + increment).astype(jnp.bfloat16), analysed)
        target = jnp.where(col_valid, col_index, COLUMNS)
        result = result.at[target].set(analysed, mode='drop')
        return (result, None)
    result, _ = lax.scan(visit_owner, jnp.zeros_like(background), jnp.arange(num_owners, dtype=jnp.int32))
    return result
```

```python
import jax
import jax.numpy as jnp
from jax import lax
from jax.experimental import pallas as pl
from jax.experimental.pallas import tpu as pltpu
from jax.sharding import PartitionSpec as P

AXES = ("gx", "gy")
PATCH_DEV = 2
OCAP = 4
CAP = 2
META = 128
MIB = 1024 * 1024
F32 = jnp.float32
BF16 = jnp.bfloat16


def ranks(owner, owners):
    n = owner.shape[1]
    onehot = lax.broadcasted_iota(jnp.int32, (owners, n), 0) == owner
    earlier = lax.broadcasted_iota(jnp.int32, (n, n), 0) < lax.broadcasted_iota(jnp.int32, (n, n), 1)
    before = jnp.dot(
        onehot.astype(F32).astype(BF16), earlier.astype(F32).astype(BF16), preferred_element_type=F32
    )
    rank = jnp.sum(jnp.where(onehot, before, 0.0), axis=0, keepdims=True)
    return rank.astype(jnp.int32)


def pack_rows_kernel(pert_ref, innov_ref, rinv_ref, loc_ref, patch_ref, target_ref, out_ref, slot_ref):
    obs, members = pert_ref.shape
    slots = out_ref.shape[0]
    owners = slots // OCAP
    patch = jnp.concatenate([patch_ref[0:1, :], patch_ref[1:2, :]], axis=1)
    owner = patch >> 1
    entry_slot = owner * OCAP + ranks(owner, owners)
    root = jnp.sqrt(rinv_ref[...] * loc_ref[...])
    lifted = (root * innov_ref[...]).astype(BF16).astype(F32)
    root = jnp.concatenate([root[0:1, :], root[1:2, :]], axis=1)
    lifted = jnp.concatenate([lifted[0:1, :], lifted[1:2, :]], axis=1)
    tag = ((patch & 1) + 1).astype(F32)

    target = target_ref[...]
    col_owner = target >> 1
    col_rank = ranks(col_owner, owners)
    slot_ref[...] = col_owner * CAP + col_rank
    col_slot = col_owner * OCAP + col_rank
    col_tag = ((target & 1) + 1).astype(F32)

    chosen = lax.broadcasted_iota(jnp.int32, (slots, 2 * obs), 0) == entry_slot
    col_chosen = lax.broadcasted_iota(jnp.int32, (slots, target.shape[1]), 0) == col_slot

    def pick(mask, values):
        return jnp.sum(jnp.where(mask, values, 0.0), axis=1, keepdims=True)

    pick_rows = chosen.astype(F32)
    pick_rows = (pick_rows[:, :obs] + pick_rows[:, obs:]).astype(BF16)
    rows = jnp.dot(pick_rows, pert_ref[...], preferred_element_type=F32)
    out_ref[:, :members] = (rows * pick(chosen, root)).astype(BF16)
    lane = lax.broadcasted_iota(jnp.int32, (slots, META), 1)
    meta = jnp.where(lane == 0, pick(chosen, lifted), 0.0)
    meta = jnp.where(lane == 1, pick(chosen, tag), meta)
    meta = jnp.where(lane == 2, pick(col_chosen, col_tag), meta)
    out_ref[:, members:] = meta.astype(BF16)


def pack_cols_kernel(slot_ref, cols_ref, out_ref, sem):
    count = cols_ref.shape[0]

    def start(i, carry):
        pltpu.make_async_copy(cols_ref.at[i], out_ref.at[slot_ref[0, i]], sem).start()
        return carry

    lax.fori_loop(0, count, start, 0, unroll=8)
    pltpu.make_async_copy(cols_ref, out_ref.at[pl.ds(0, count)], sem).wait()


def unpack_cols_kernel(slot_ref, cols_ref, out_ref, sem):
    count = out_ref.shape[0]

    def start(i, carry):
        pltpu.make_async_copy(cols_ref.at[slot_ref[0, i]], out_ref.at[i], sem).start()
        return carry

    lax.fori_loop(0, count, start, 0, unroll=8)
    pltpu.make_async_copy(cols_ref.at[pl.ds(0, count)], out_ref, sem).wait()


def split(x):
    high = x.astype(BF16)
    return high, (x - high.astype(F32)).astype(BF16)


def product(a, b):
    (ah, al), (bh, bl) = a, b
    return (
        jnp.dot(ah, bh, preferred_element_type=F32)
        + jnp.dot(ah, bl, preferred_element_type=F32)
        + jnp.dot(al, bh, preferred_element_type=F32)
    )


def two_steps(x, diagonal):
    parts = split(x)
    square = product(parts, parts)
    inner = 0.0625 * square - 0.5625 * x + 1.6875 * diagonal
    return product(split(inner), split(square)) - 2.4375 * x + 2.25 * diagonal


def weights_kernel(rows_ref, out_ref):
    members = out_ref.shape[1]
    meta = rows_ref[:, members:].astype(F32)
    tag = meta[:, 1:2]
    rows = rows_ref[...].astype(F32)
    diagonal = (
        lax.broadcasted_iota(jnp.int32, (members, members), 0)
        == lax.broadcasted_iota(jnp.int32, (members, members), 1)
    ).astype(F32)
    for patch in range(PATCH_DEV):
        masked = jnp.where(tag == patch + 1, rows, 0.0).astype(BF16)
        wide = lax.dot_general(
            masked[:, :members], masked, (((0,), (0,)), ((), ())), preferred_element_type=F32
        )
        pull = wide[:, members : members + 1]
        system = wide[:, :members] + (members - 1) * diagonal
        bound = jnp.max(jnp.sum(jnp.abs(system), axis=0, keepdims=True), axis=1, keepdims=True)
        scale = 1.0 / bound
        current = system * scale
        half = two_steps(current, diagonal)
        half_parts = split(half)
        later = product(split(product(half_parts, half_parts)), split(current))
        inverse = product(half_parts, split(two_steps(later, diagonal)))
        once = jnp.sum(inverse * pull, axis=0, keepdims=True)
        mean_weight = jnp.sum(inverse * once, axis=1, keepdims=True) * scale
        out_ref[patch] = (jnp.sqrt((members - 1) * scale) * inverse + mean_weight).astype(BF16)


def apply_kernel(cols_ref, tag_ref, weights_ref, out_ref):
    slots, levels, members = cols_ref.shape
    widened = cols_ref[...].astype(F32)
    mean = jnp.mean(widened, axis=-1, keepdims=True)
    spread = (widened - mean).reshape(slots * levels, members).astype(BF16)
    first = jnp.dot(spread, weights_ref[0], preferred_element_type=F32)
    second = jnp.dot(spread, weights_ref[1], preferred_element_type=F32)
    is_second = tag_ref[...].reshape(slots * levels, -1)[:, 0:1] == 2.0
    increment = jnp.where(is_second, second, first).reshape(slots, levels, members)
    out_ref[...] = (mean + increment).astype(BF16)


def exchange(x):
    return lax.all_to_all(x, AXES, split_axis=0, concat_axis=0, tiled=True)


VMEM = pl.BlockSpec(memory_space=pltpu.VMEM)
SMEM = pl.BlockSpec(memory_space=pltpu.SMEM)
ANY = pl.BlockSpec(memory_space=pl.ANY)


def on_device(background, col_target, obs_pert, innovation, obs_rinv, obs_loc, obs_patch):
    owners = lax.axis_size(AXES)
    cols, levels, members = background.shape
    width = members + META
    payload, col_slot = pl.pallas_call(
        pack_rows_kernel,
        out_shape=(
            jax.ShapeDtypeStruct((owners * OCAP, width), BF16),
            jax.ShapeDtypeStruct((1, cols), jnp.int32),
        ),
        in_specs=[VMEM] * 6,
        out_specs=(VMEM, VMEM),
        name="pack_rows",
    )(
        obs_pert,
        innovation[None, :],
        obs_rinv[None, :],
        obs_loc,
        obs_patch,
        col_target[None, :],
    )
    payload = exchange(payload.reshape(owners, OCAP, width))

    send = pl.pallas_call(
        pack_cols_kernel,
        out_shape=jax.ShapeDtypeStruct((owners * CAP, levels, members), BF16),
        in_specs=[SMEM, ANY],
        out_specs=ANY,
        scratch_shapes=[pltpu.SemaphoreType.DMA],
        name="pack_cols",
        cost_estimate=pl.CostEstimate(flops=0, bytes_accessed=6 * MIB, transcendentals=0),
    )(col_slot, background)
    received = exchange(send.reshape(owners, CAP, levels, members)).reshape(send.shape)

    weights = pl.pallas_call(
        weights_kernel,
        out_shape=jax.ShapeDtypeStruct((PATCH_DEV, members, members), BF16),
        in_specs=[VMEM],
        out_specs=VMEM,
        compiler_params=pltpu.CompilerParams(vmem_limit_bytes=40 * MIB),
        name="weights",
        cost_estimate=pl.CostEstimate(
            flops=2 * 2 * 23 * members**3, bytes_accessed=2 * MIB, transcendentals=0
        ),
    )(payload.reshape(owners * OCAP, width))
    tags = jnp.broadcast_to(
        payload[:, :CAP, members + 2].astype(F32).reshape(owners * CAP, 1, 1),
        (owners * CAP, levels, 128),
    )

    block = 32
    analysed = pl.pallas_call(
        apply_kernel,
        out_shape=jax.ShapeDtypeStruct(send.shape, BF16),
        grid=(send.shape[0] // block,),
        in_specs=[
            pl.BlockSpec((block, levels, members), lambda i: (i, 0, 0)),
            pl.BlockSpec((block, levels, 128), lambda i: (i, 0, 0)),
            pl.BlockSpec((PATCH_DEV, members, members), lambda i: (0, 0, 0)),
        ],
        out_specs=pl.BlockSpec((block, levels, members), lambda i: (i, 0, 0)),
        compiler_params=pltpu.CompilerParams(vmem_limit_bytes=32 * MIB),
        name="apply_weights",
    )(received, tags, weights)

    returned = exchange(analysed.reshape(owners, CAP, levels, members)).reshape(send.shape)
    return pl.pallas_call(
        unpack_cols_kernel,
        out_shape=jax.ShapeDtypeStruct(background.shape, BF16),
        in_specs=[SMEM, ANY],
        out_specs=ANY,
        scratch_shapes=[pltpu.SemaphoreType.DMA],
        name="unpack_cols",
    )(col_slot, returned)


def solution(mesh):
    return jax.shard_map(
        on_device,
        mesh=mesh,
        in_specs=(
            P(AXES, None, None),
            P(AXES),
            P(AXES, None),
            P(AXES),
            P(AXES),
            P(None, AXES),
            P(None, AXES),
        ),
        out_specs=P(AXES, None, None),
        check_vma=False,
    )
```

```python
import jax
import jax.numpy as jnp
from jax import lax
from jax.experimental import pallas as pl
from jax.experimental.pallas import tpu as pltpu
from jax.sharding import PartitionSpec as P

AXES = ("gx", "gy")
PATCH_DEV = 2
OCAP = 4
CAP = 2
META = 128
MIB = 1024 * 1024
F32 = jnp.float32
BF16 = jnp.bfloat16


def ranks(owner, owners):
    n = owner.shape[1]
    onehot = lax.broadcasted_iota(jnp.int32, (owners, n), 0) == owner
    earlier = lax.broadcasted_iota(jnp.int32, (n, n), 0) < lax.broadcasted_iota(jnp.int32, (n, n), 1)
    before = jnp.dot(
        onehot.astype(F32).astype(BF16), earlier.astype(F32).astype(BF16), preferred_element_type=F32
    )
    rank = jnp.sum(jnp.where(onehot, before, 0.0), axis=0, keepdims=True)
    return rank.astype(jnp.int32)


def pack_rows_kernel(pert_ref, innov_ref, rinv_ref, loc_ref, patch_ref, target_ref, out_ref, slot_ref):
    obs, members = pert_ref.shape
    owners = out_ref.shape[0]
    padded = 8 * owners
    patch = jnp.concatenate([patch_ref[0:1, :], patch_ref[1:2, :]], axis=1)
    owner = patch >> 1
    entry_slot = owner * 8 + ranks(owner, owners)
    root = jnp.sqrt(rinv_ref[...] * loc_ref[...])
    lifted = (root * innov_ref[...]).astype(BF16).astype(F32)
    root = jnp.concatenate([root[0:1, :], root[1:2, :]], axis=1)
    lifted = jnp.concatenate([lifted[0:1, :], lifted[1:2, :]], axis=1)
    tag = ((patch & 1) + 1).astype(F32)

    target = target_ref[...]
    col_owner = target >> 1
    col_rank = ranks(col_owner, owners)
    slot_ref[...] = col_owner * CAP + col_rank
    col_slot = col_owner * 8 + col_rank
    col_tag = ((target & 1) + 1).astype(F32)

    chosen = lax.broadcasted_iota(jnp.int32, (padded, 2 * obs), 0) == entry_slot
    col_chosen = lax.broadcasted_iota(jnp.int32, (padded, target.shape[1]), 0) == col_slot

    def pick(mask, values):
        return jnp.sum(jnp.where(mask, values, 0.0), axis=1, keepdims=True)

    pick_rows = chosen.astype(F32)
    pick_rows = (pick_rows[:, :obs] + pick_rows[:, obs:]).astype(BF16)
    rows = jnp.dot(pick_rows, pert_ref[...], preferred_element_type=F32)
    rows = rows * pick(chosen, root)
    out_ref[:, :, :members] = rows.reshape(owners, 8, members)[:, :OCAP].astype(BF16)
    lane = lax.broadcasted_iota(jnp.int32, (padded, META), 1)
    meta = jnp.where(lane == 0, pick(chosen, lifted), 0.0)
    meta = jnp.where(lane == 1, pick(chosen, tag), meta)
    meta = jnp.where(lane == 2, pick(col_chosen, col_tag), meta)
    out_ref[:, :, members:] = meta.reshape(owners, 8, META)[:, :OCAP].astype(BF16)


def pack_cols_kernel(slot_ref, cols_ref, out_ref):
    def place(i, carry):
        out_ref[slot_ref[0, i]] = cols_ref[i]
        return carry

    lax.fori_loop(0, cols_ref.shape[0], place, 0, unroll=8)


def unpack_cols_kernel(slot_ref, cols_ref, out_ref):
    block = out_ref.shape[0]
    first = pl.program_id(0) * block

    def place(i, carry):
        out_ref[i] = cols_ref[slot_ref[0, first + i]]
        return carry

    lax.fori_loop(0, block, place, 0, unroll=8)


def split(x):
    high = x.astype(BF16)
    return high, (x - high.astype(F32)).astype(BF16)


def product(a, b):
    (ah, al), (bh, bl) = a, b
    return (
        jnp.dot(ah, bh, preferred_element_type=F32)
        + jnp.dot(ah, bl, preferred_element_type=F32)
        + jnp.dot(al, bh, preferred_element_type=F32)
    )


def two_steps(x, diagonal):
    parts = split(x)
    square = product(parts, parts)
    inner = 0.0625 * square - 0.5625 * x + 1.6875 * diagonal
    return product(split(inner), split(square)) - 2.4375 * x + 2.25 * diagonal


def weights_kernel(rows_ref, out_ref):
    members = out_ref.shape[1]
    meta = rows_ref[:, members:].astype(F32)
    tag = meta[:, 1:2]
    rows = rows_ref[...].astype(F32)
    diagonal = (
        lax.broadcasted_iota(jnp.int32, (members, members), 0)
        == lax.broadcasted_iota(jnp.int32, (members, members), 1)
    ).astype(F32)
    for patch in range(PATCH_DEV):
        masked = jnp.where(tag == patch + 1, rows, 0.0).astype(BF16)
        wide = lax.dot_general(
            masked[:, :members], masked, (((0,), (0,)), ((), ())), preferred_element_type=F32
        )
        pull = wide[:, members : members + 1]
        system = wide[:, :members] + (members - 1) * diagonal
        bound = jnp.max(jnp.sum(jnp.abs(system), axis=0, keepdims=True), axis=1, keepdims=True)
        scale = 1.0 / bound
        current = system * scale
        half = two_steps(current, diagonal)
        half_parts = split(half)
        later = product(split(product(half_parts, half_parts)), split(current))
        inverse = product(half_parts, split(two_steps(later, diagonal)))
        once = jnp.sum(inverse * pull, axis=0, keepdims=True)
        mean_weight = jnp.sum(inverse * once, axis=1, keepdims=True) * scale
        out_ref[patch] = (jnp.sqrt((members - 1) * scale) * inverse + mean_weight).astype(BF16)


def apply_kernel(cols_ref, tag_ref, weights_ref, out_ref):
    slots, levels, members = cols_ref.shape
    widened = cols_ref[...].astype(F32)
    mean = jnp.mean(widened, axis=-1, keepdims=True)
    spread = (widened - mean).reshape(slots * levels, members).astype(BF16)
    first = jnp.dot(spread, weights_ref[0], preferred_element_type=F32)
    second = jnp.dot(spread, weights_ref[1], preferred_element_type=F32)
    is_second = tag_ref[...].reshape(slots * levels, -1)[:, 0:1] == 2.0
    increment = jnp.where(is_second, second, first).reshape(slots, levels, members)
    out_ref[...] = (mean + increment).astype(BF16)


def exchange(x):
    return lax.all_to_all(x, AXES, split_axis=0, concat_axis=0, tiled=True)


VMEM = pl.BlockSpec(memory_space=pltpu.VMEM)
SMEM = pl.BlockSpec(memory_space=pltpu.SMEM)


def on_device(background, col_target, obs_pert, innovation, obs_rinv, obs_loc, obs_patch):
    owners = lax.axis_size(AXES)
    cols, levels, members = background.shape
    width = members + META
    payload, col_slot = pl.pallas_call(
        pack_rows_kernel,
        out_shape=(
            jax.ShapeDtypeStruct((owners, OCAP, width), BF16),
            jax.ShapeDtypeStruct((1, cols), jnp.int32),
        ),
        in_specs=[VMEM] * 6,
        out_specs=(VMEM, VMEM),
        name="pack_rows",
    )(
        obs_pert,
        innovation[None, :],
        obs_rinv[None, :],
        obs_loc,
        obs_patch,
        col_target[None, :],
    )
    payload = exchange(payload)

    send = pl.pallas_call(
        pack_cols_kernel,
        out_shape=jax.ShapeDtypeStruct((owners * CAP, levels, members), BF16),
        in_specs=[SMEM, VMEM],
        out_specs=VMEM,
        name="pack_cols",
        cost_estimate=pl.CostEstimate(flops=0, bytes_accessed=6 * MIB, transcendentals=0),
    )(col_slot, background)
    received = exchange(send.reshape(owners, CAP, levels, members)).reshape(send.shape)

    weights = pl.pallas_call(
        weights_kernel,
        out_shape=jax.ShapeDtypeStruct((PATCH_DEV, members, members), BF16),
        in_specs=[VMEM],
        out_specs=VMEM,
        compiler_params=pltpu.CompilerParams(vmem_limit_bytes=40 * MIB),
        name="weights",
        cost_estimate=pl.CostEstimate(
            flops=2 * 2 * 23 * members**3, bytes_accessed=2 * MIB, transcendentals=0
        ),
    )(payload.reshape(owners * OCAP, width))
    tags = jnp.broadcast_to(
        payload[:, :CAP, members + 2].astype(F32).reshape(owners * CAP, 1, 1),
        (owners * CAP, levels, 128),
    )

    block = 32
    analysed = pl.pallas_call(
        apply_kernel,
        out_shape=jax.ShapeDtypeStruct(send.shape, BF16),
        grid=(send.shape[0] // block,),
        in_specs=[
            pl.BlockSpec((block, levels, members), lambda i: (i, 0, 0)),
            pl.BlockSpec((block, levels, 128), lambda i: (i, 0, 0)),
            pl.BlockSpec((PATCH_DEV, members, members), lambda i: (0, 0, 0)),
        ],
        out_specs=pl.BlockSpec((block, levels, members), lambda i: (i, 0, 0)),
        compiler_params=pltpu.CompilerParams(vmem_limit_bytes=32 * MIB),
        name="apply_weights",
    )(received, tags, weights)

    returned = exchange(analysed.reshape(owners, CAP, levels, members)).reshape(send.shape)
    return pl.pallas_call(
        unpack_cols_kernel,
        out_shape=jax.ShapeDtypeStruct(background.shape, BF16),
        grid=(cols // block,),
        in_specs=[SMEM, VMEM],
        out_specs=pl.BlockSpec((block, levels, members), lambda i: (i, 0, 0)),
        name="unpack_cols",
    )(col_slot, returned)


def solution(mesh):
    return jax.shard_map(
        on_device,
        mesh=mesh,
        in_specs=(
            P(AXES, None, None),
            P(AXES),
            P(AXES, None),
            P(AXES),
            P(AXES),
            P(None, AXES),
            P(None, AXES),
        ),
        out_specs=P(AXES, None, None),
        check_vma=False,
    )
```

```python
import jax
import jax.numpy as jnp
from jax import lax
from jax.experimental import pallas as pl
from jax.experimental.pallas import tpu as pltpu
from jax.sharding import PartitionSpec as P

AXES = ("gx", "gy")
PATCH_DEV = 2
OCAP = 4
CAP = 2
META = 128
MIB = 1024 * 1024
F32 = jnp.float32
BF16 = jnp.bfloat16


def ranks(owner, owners):
    n = owner.shape[1]
    onehot = lax.broadcasted_iota(jnp.int32, (owners, n), 0) == owner
    earlier = lax.broadcasted_iota(jnp.int32, (n, n), 0) < lax.broadcasted_iota(jnp.int32, (n, n), 1)
    before = jnp.dot(
        jnp.where(onehot, 1.0, 0.0).astype(BF16),
        jnp.where(earlier, 1.0, 0.0).astype(BF16),
        preferred_element_type=F32,
    )
    rank = jnp.sum(jnp.where(onehot, before, 0.0), axis=0, keepdims=True)
    return rank.astype(jnp.int32)


def pack_kernel(
    pert_ref, innov_ref, rinv_ref, loc_ref, patch_ref, target_ref, cols_ref, out_ref, slot_ref,
    held_cols, held_slot, cols_sem, slot_sem,
):
    obs, members = pert_ref.shape
    owners = out_ref.shape[0]
    cols = cols_ref.shape[0]
    half = members // 2
    cols_copy = pltpu.make_async_copy(cols_ref, held_cols, cols_sem)
    cols_copy.start()

    target = target_ref[...]
    col_owner = target >> 1
    col_rank = ranks(col_owner, owners)
    slot_ref[...] = col_owner * CAP + col_rank
    slot_copy = pltpu.make_async_copy(slot_ref, held_slot, slot_sem)
    slot_copy.start()

    patch = jnp.concatenate([patch_ref[0:1, :], patch_ref[1:2, :]], axis=1)
    owner = patch >> 1
    entry_slot = owner * 8 + ranks(owner, owners)
    root = jnp.sqrt(rinv_ref[...] * loc_ref[...])
    lifted = root * innov_ref[...]
    root = jnp.concatenate([root[0:1, :], root[1:2, :]], axis=1)
    lifted = jnp.concatenate([lifted[0:1, :], lifted[1:2, :]], axis=1)
    tag = ((patch & 1) + 1).astype(F32)
    col_tag = ((target & 1) + 1).astype(F32)
    col_tags = [jnp.where(col_rank == place, col_tag, 0.0) for place in range(CAP)]
    col_tags = [jnp.concatenate([t, jnp.zeros((1, 2 * obs - cols), F32)], axis=1) for t in col_tags]
    by_entry = jnp.concatenate([root, lifted, tag, *col_tags, jnp.zeros((3, 2 * obs), F32)], axis=0).T

    pert = pert_ref[...].astype(F32)
    rows = (jnp.concatenate([pert, pert], axis=0) * by_entry[:, 0:1]).astype(BF16)
    lane = lax.broadcasted_iota(jnp.int32, (2 * obs, META), 1)
    meta = jnp.where(lane == 0, by_entry[:, 1:2], jnp.where(lane == 1, by_entry[:, 2:3], 0.0))
    lane = lax.broadcasted_iota(jnp.int32, (cols, META), 1)
    col_meta = jnp.where(
        lane == 2, by_entry[:cols, 3:4], jnp.where(lane == 3, by_entry[:cols, 4:5], 0.0)
    )

    place = lax.broadcasted_iota(jnp.int32, (8 * owners, 2 * obs), 0)
    chosen = jnp.where((place & ~OCAP) == entry_slot, 1.0, 0.0).astype(BF16)
    place = lax.broadcasted_iota(jnp.int32, (8 * owners, cols), 0)
    col_chosen = jnp.where((place >> 3) == col_owner, 1.0, 0.0).astype(BF16)
    place = lax.broadcasted_iota(jnp.int32, (8 * owners, half), 0)
    packed = jnp.where(
        (place & OCAP) == 0,
        jnp.dot(chosen, rows[:, :half], preferred_element_type=F32),
        jnp.dot(chosen, rows[:, half:], preferred_element_type=F32),
    )
    out_ref[:, :, 2 * members : 2 * members + half] = packed.reshape(owners, 8, half).astype(BF16)
    packed = jnp.dot(chosen, meta.astype(BF16), preferred_element_type=F32)
    packed += jnp.dot(col_chosen, col_meta.astype(BF16), preferred_element_type=F32)
    out_ref[:, :, 2 * members + half :] = packed.reshape(owners, 8, META).astype(BF16)

    slot_copy.wait()
    cols_copy.wait()

    def put(i, carry):
        slot = held_slot[0, i]
        lanes = pl.ds(pl.multiple_of((slot & 1) * members, members), members)
        out_ref[slot >> 1, :, lanes] = held_cols[i]
        return carry

    lax.fori_loop(0, cols, put, 0, unroll=8)


def unpack_kernel(slot_ref, cols_ref, out_ref):
    block, _, members = out_ref.shape
    first = pl.program_id(0) * block

    def take(i, carry):
        slot = slot_ref[0, first + i]
        lanes = pl.ds(pl.multiple_of((slot & 1) * members, members), members)
        out_ref[i] = cols_ref[slot >> 1, :, lanes]
        return carry

    lax.fori_loop(0, block, take, 0, unroll=8)


def product(a, b):
    return jnp.dot(a.astype(BF16), b.astype(BF16), preferred_element_type=F32)


def two_steps(c, b):
    y = 2.25 + c * (-2.4375 + c * (1.6875 + c * (-0.5625 + c * 0.0625)))
    first = -2.4375 + c * (3.375 + c * (-1.6875 + c * 0.25))
    second = 1.6875 + c * (-1.6875 + c * 0.375)
    third = -0.5625 + c * 0.25
    square = product(b, b)
    return y, product(0.0625 * square + third * b, square) + second * square + first * b


def analyse_kernel(payload_ref, out_ref, weights_ref):
    sources, levels, _ = payload_ref.shape
    members = weights_ref.shape[1]
    half = members // 2
    rows = payload_ref[:, :, 2 * members :].astype(F32).reshape(sources // 2, 2, 8, half + META)
    even, odd = rows[:, 0], rows[:, 1]

    def together(lanes, first):
        pair = [even[:, first : first + OCAP, lanes], odd[:, first : first + OCAP, lanes]]
        return jnp.concatenate(pair, axis=1).reshape(sources * OCAP, -1)

    meta = together(slice(half, half + META), 0)
    tag = meta[:, 1:2]
    rows = jnp.concatenate([together(slice(0, half), 0), together(slice(0, half), OCAP), meta], axis=1)
    diagonal = lax.broadcasted_iota(jnp.int32, (members, members), 0) == lax.broadcasted_iota(
        jnp.int32, (members, members), 1
    )
    for patch in range(PATCH_DEV):
        masked = jnp.where(tag == patch + 1, rows, 0.0).astype(BF16)
        wide = lax.dot_general(
            masked[:, :members], masked, (((0,), (0,)), ((), ())), preferred_element_type=F32
        )
        pull = wide[:, members : members + 1]
        gram = wide[:, :members]
        bound = (members - 1) + jnp.max(
            jnp.sum(jnp.abs(gram), axis=0, keepdims=True), axis=1, keepdims=True
        )
        trace = jnp.sum(jnp.sum(jnp.where(diagonal, gram, 0.0), axis=0, keepdims=True), axis=1, keepdims=True)
        scale = 1.0 / bound
        c = (trace / members + (members - 1)) * scale
        b = gram * scale + jnp.where(diagonal, (members - 1) * scale - c, 0.0)
        z, d = two_steps(c, b)
        u = 2.0 * z * d + product(d, d)
        q = product(u, b) + z * z * b + c * u
        y, f = two_steps(z * z * c, q)
        inverse = product(d, f) + z * f + y * d + jnp.where(diagonal, z * y, 0.0)
        once = jnp.sum(inverse * pull, axis=0, keepdims=True)
        mean_weight = jnp.sum(inverse * once, axis=1, keepdims=True) * scale
        weights_ref[patch] = (jnp.sqrt((members - 1) * scale) * inverse + mean_weight).astype(BF16)

    block = 32
    for place in range(CAP):
        lanes = pl.ds(place * members, members)
        tag_lane = 2 * members + half + 2 + place

        def apply(i, carry):
            some = pl.ds(pl.multiple_of(i * block, block), block)
            widened = payload_ref[some, :, lanes].astype(F32)
            mean = jnp.mean(widened, axis=-1, keepdims=True)
            spread = (widened - mean).reshape(block * levels, members).astype(BF16)
            first = jnp.dot(spread, weights_ref[0], preferred_element_type=F32)
            second = jnp.dot(spread, weights_ref[1], preferred_element_type=F32)
            tags = payload_ref[some, :, pl.ds(2 * members + half, META)].astype(F32)
            tags = tags.reshape(block * levels, META)[:, 2 + place : 3 + place]
            increment = jnp.where(tags == 2.0, second, first).reshape(block, levels, members)
            out_ref[some, :, lanes] = (mean + increment).astype(BF16)
            return carry

        lax.fori_loop(0, sources // block, apply, 0)


def exchange(x):
    return lax.all_to_all(x, AXES, split_axis=0, concat_axis=0, tiled=True)


VMEM = pl.BlockSpec(memory_space=pltpu.VMEM)
SMEM = pl.BlockSpec(memory_space=pltpu.SMEM)
ANY = pl.BlockSpec(memory_space=pl.ANY)


def on_device(background, col_target, obs_pert, innovation, obs_rinv, obs_loc, obs_patch):
    owners = lax.axis_size(AXES)
    cols, levels, members = background.shape
    width = 2 * members + members // 2 + META
    payload, col_slot = pl.pallas_call(
        pack_kernel,
        out_shape=(
            jax.ShapeDtypeStruct((owners, levels, width), BF16),
            jax.ShapeDtypeStruct((1, cols), jnp.int32),
        ),
        in_specs=[VMEM] * 6 + [ANY],
        out_specs=(VMEM, VMEM),
        scratch_shapes=[
            pltpu.VMEM(background.shape, BF16),
            pltpu.SMEM((1, cols), jnp.int32),
            pltpu.SemaphoreType.DMA,
            pltpu.SemaphoreType.DMA,
        ],
        compiler_params=pltpu.CompilerParams(vmem_limit_bytes=32 * MIB),
        name="pack",
    )(
        obs_pert,
        innovation[None, :],
        obs_rinv[None, :],
        obs_loc,
        obs_patch,
        col_target[None, :],
        background,
    )
    payload = exchange(payload)

    analysed = pl.pallas_call(
        analyse_kernel,
        out_shape=jax.ShapeDtypeStruct((owners, levels, CAP * members), BF16),
        in_specs=[VMEM],
        out_specs=VMEM,
        scratch_shapes=[pltpu.VMEM((PATCH_DEV, members, members), BF16)],
        compiler_params=pltpu.CompilerParams(vmem_limit_bytes=40 * MIB),
        name="analyse",
    )(payload)
    returned = exchange(analysed)

    block = 32
    return pl.pallas_call(
        unpack_kernel,
        out_shape=jax.ShapeDtypeStruct(background.shape, BF16),
        grid=(cols // block,),
        in_specs=[SMEM, VMEM],
        out_specs=pl.BlockSpec((block, levels, members), lambda i: (i, 0, 0)),
        name="unpack",
    )(col_slot, returned)


def solution(mesh):
    return jax.shard_map(
        on_device,
        mesh=mesh,
        in_specs=(
            P(AXES, None, None),
            P(AXES),
            P(AXES, None),
            P(AXES),
            P(AXES),
            P(None, AXES),
            P(None, AXES),
        ),
        out_specs=P(AXES, None, None),
        check_vma=False,
    )
```

```python
import jax
import jax.numpy as jnp
from jax import lax
from jax.experimental import pallas as pl
from jax.experimental.pallas import tpu as pltpu
from jax.sharding import PartitionSpec as P

AXES = ("gx", "gy")
PATCH_DEV = 2
OCAP = 4
CAP = 2
META = 128
MIB = 1024 * 1024
F32 = jnp.float32
BF16 = jnp.bfloat16


def ranks(owner, owners):
    n = owner.shape[1]
    onehot = lax.broadcasted_iota(jnp.int32, (owners, n), 0) == owner
    earlier = lax.broadcasted_iota(jnp.int32, (n, n), 0) < lax.broadcasted_iota(jnp.int32, (n, n), 1)
    before = jnp.dot(
        jnp.where(onehot, 1.0, 0.0).astype(BF16),
        jnp.where(earlier, 1.0, 0.0).astype(BF16),
        preferred_element_type=F32,
    )
    rank = jnp.sum(jnp.where(onehot, before, 0.0), axis=0, keepdims=True)
    return rank.astype(jnp.int32)


def pack_kernel(
    pert_hbm, innov_hbm, rinv_hbm, loc_hbm, patch_hbm, target_hbm, cols_hbm, out_ref, slot_hbm,
    pert_ref, innov_ref, rinv_ref, loc_ref, patch_ref, target_ref, held_cols, slot_ref, held_slot, sems,
):
    obs, members = pert_ref.shape
    owners = out_ref.shape[0]
    cols = held_cols.shape[0]
    half = members // 2
    pairs = (
        (target_hbm, target_ref), (patch_hbm, patch_ref), (rinv_hbm, rinv_ref), (loc_hbm, loc_ref),
        (innov_hbm, innov_ref), (pert_hbm, pert_ref), (cols_hbm, held_cols),
    )
    copies = [pltpu.make_async_copy(*pair, sems.at[i]) for i, pair in enumerate(pairs)]
    for copy in copies:
        copy.start()
    target_copy, *row_copies, cols_copy = copies
    target_copy.wait()

    target = target_ref[...]
    col_owner = target >> 1
    col_rank = ranks(col_owner, owners)
    slot_ref[...] = col_owner * CAP + col_rank
    slot_copies = [
        pltpu.make_async_copy(slot_ref, held_slot, sems.at[7]),
        pltpu.make_async_copy(slot_ref, slot_hbm, sems.at[8]),
    ]
    for copy in slot_copies:
        copy.start()
    for copy in row_copies:
        copy.wait()

    patch = jnp.concatenate([patch_ref[0:1, :], patch_ref[1:2, :]], axis=1)
    owner = patch >> 1
    entry_slot = owner * 8 + ranks(owner, owners)
    root = jnp.sqrt(rinv_ref[...] * loc_ref[...])
    lifted = root * innov_ref[...]
    root = jnp.concatenate([root[0:1, :], root[1:2, :]], axis=1)
    lifted = jnp.concatenate([lifted[0:1, :], lifted[1:2, :]], axis=1)
    tag = ((patch & 1) + 1).astype(F32)
    col_tag = ((target & 1) + 1).astype(F32)
    col_tags = [jnp.where(col_rank == place, col_tag, 0.0) for place in range(CAP)]
    col_tags = [jnp.concatenate([t, jnp.zeros((1, 2 * obs - cols), F32)], axis=1) for t in col_tags]
    by_entry = jnp.concatenate([root, lifted, tag, *col_tags, jnp.zeros((3, 2 * obs), F32)], axis=0).T

    pert = pert_ref[...].astype(F32)
    rows = (jnp.concatenate([pert, pert], axis=0) * by_entry[:, 0:1]).astype(BF16)
    lane = lax.broadcasted_iota(jnp.int32, (2 * obs, META), 1)
    meta = jnp.where(lane == 0, by_entry[:, 1:2], jnp.where(lane == 1, by_entry[:, 2:3], 0.0))
    lane = lax.broadcasted_iota(jnp.int32, (cols, META), 1)
    col_meta = jnp.where(
        lane == 2, by_entry[:cols, 3:4], jnp.where(lane == 3, by_entry[:cols, 4:5], 0.0)
    )

    place = lax.broadcasted_iota(jnp.int32, (8 * owners, 2 * obs), 0)
    chosen = jnp.where((place & ~OCAP) == entry_slot, 1.0, 0.0).astype(BF16)
    place = lax.broadcasted_iota(jnp.int32, (8 * owners, cols), 0)
    col_chosen = jnp.where((place >> 3) == col_owner, 1.0, 0.0).astype(BF16)
    place = lax.broadcasted_iota(jnp.int32, (8 * owners, half), 0)
    packed = jnp.where(
        (place & OCAP) == 0,
        jnp.dot(chosen, rows[:, :half], preferred_element_type=F32),
        jnp.dot(chosen, rows[:, half:], preferred_element_type=F32),
    )
    out_ref[:, :, 2 * members : 2 * members + half] = packed.reshape(owners, 8, half).astype(BF16)
    packed = jnp.dot(chosen, meta.astype(BF16), preferred_element_type=F32)
    packed += jnp.dot(col_chosen, col_meta.astype(BF16), preferred_element_type=F32)
    out_ref[:, :, 2 * members + half :] = packed.reshape(owners, 8, META).astype(BF16)

    for copy in slot_copies:
        copy.wait()
    cols_copy.wait()

    def put(i, carry):
        slot = held_slot[0, i]
        lanes = pl.ds(pl.multiple_of((slot & 1) * members, members), members)
        out_ref[slot >> 1, :, lanes] = held_cols[i]
        return carry

    lax.fori_loop(0, cols, put, 0, unroll=8)


def unpack_kernel(slot_ref, cols_ref, out_hbm, held_cols, sems):
    cols, _, members = held_cols.shape
    chunks = sems.shape[0]
    block = cols // chunks
    copies = []
    for chunk in range(chunks):

        def take(i, carry):
            slot = slot_ref[0, i]
            lanes = pl.ds(pl.multiple_of((slot & 1) * members, members), members)
            held_cols[i] = cols_ref[slot >> 1, :, lanes]
            return carry

        lax.fori_loop(chunk * block, (chunk + 1) * block, take, 0, unroll=8)
        some = pl.ds(chunk * block, block)
        copies.append(pltpu.make_async_copy(held_cols.at[some], out_hbm.at[some], sems.at[chunk]))
        copies[-1].start()
    for copy in copies:
        copy.wait()


def product(a, b):
    return jnp.dot(a.astype(BF16), b.astype(BF16), preferred_element_type=F32)


def products(a, b):
    return [product(x, y) for x, y in zip(a, b)]


def two_steps(c, b):
    square = products(b, b)
    y = [2.25 + x * (-2.4375 + x * (1.6875 + x * (-0.5625 + x * 0.0625))) for x in c]
    first = [-2.4375 + x * (3.375 + x * (-1.6875 + x * 0.25)) for x in c]
    second = [1.6875 + x * (-1.6875 + x * 0.375) for x in c]
    third = [-0.5625 + x * 0.25 for x in c]
    inner = [0.0625 * s + t * x for s, t, x in zip(square, third, b)]
    high = products(inner, square)
    return y, [p + t * s + o * x for p, t, s, o, x in zip(high, second, square, first, b)]


def analyse_kernel(payload_ref, out_ref, weights_ref):
    sources, levels, _ = payload_ref.shape
    members = weights_ref.shape[1]
    half = members // 2
    rows = payload_ref[:, :, 2 * members :].astype(F32).reshape(sources // 2, 2, 8, half + META)
    even, odd = rows[:, 0], rows[:, 1]

    def together(lanes, first):
        pair = [even[:, first : first + OCAP, lanes], odd[:, first : first + OCAP, lanes]]
        return jnp.concatenate(pair, axis=1).reshape(sources * OCAP, -1)

    meta = together(slice(half, half + META), 0)
    tag = meta[:, 1:2]
    rows = jnp.concatenate([together(slice(0, half), 0), together(slice(0, half), OCAP), meta], axis=1)
    diagonal = lax.broadcasted_iota(jnp.int32, (members, members), 0) == lax.broadcasted_iota(
        jnp.int32, (members, members), 1
    )
    both = range(PATCH_DEV)
    masked = [jnp.where(tag == patch + 1, rows, 0.0).astype(BF16) for patch in both]
    wide = [
        lax.dot_general(m[:, :members], m, (((0,), (0,)), ((), ())), preferred_element_type=F32)
        for m in masked
    ]
    gram = [w[:, :members] for w in wide]
    largest = [jnp.sum(jnp.abs(g), axis=0, keepdims=True) for g in gram]
    bound = [(members - 1) + jnp.max(r, axis=1, keepdims=True) for r in largest]
    trace = [jnp.sum(jnp.where(diagonal, g, 0.0), axis=0, keepdims=True) for g in gram]
    trace = [jnp.sum(t, axis=1, keepdims=True) for t in trace]
    scale = [1.0 / v for v in bound]
    c = [(t / members + (members - 1)) * v for t, v in zip(trace, scale)]
    b = [g * v + jnp.where(diagonal, (members - 1) * v - s, 0.0) for g, v, s in zip(gram, scale, c)]
    z, d = two_steps(c, b)
    u = [2.0 * zi * di + p for zi, di, p in zip(z, d, products(d, d))]
    q = [p + zi * zi * bi + ci * ui for p, zi, bi, ci, ui in zip(products(u, b), z, b, c, u)]
    y, f = two_steps([zi * zi * ci for zi, ci in zip(z, c)], q)
    last = products(d, f)
    for patch in both:
        inverse = last[patch] + z[patch] * f[patch] + y[patch] * d[patch]
        inverse += jnp.where(diagonal, z[patch] * y[patch], 0.0)
        once = jnp.sum(inverse * wide[patch][:, members : members + 1], axis=0, keepdims=True)
        mean_weight = jnp.sum(inverse * once, axis=1, keepdims=True) * scale[patch]
        root = jnp.sqrt((members - 1) * scale[patch])
        weights_ref[patch] = (root * inverse + mean_weight).astype(BF16)

    block = 128
    for place in range(CAP):
        lanes = pl.ds(place * members, members)
        tag_lane = 2 * members + half + 2 + place

        def apply(i, carry):
            some = pl.ds(pl.multiple_of(i * block, block), block)
            widened = payload_ref[some, :, lanes].astype(F32)
            mean = jnp.mean(widened, axis=-1, keepdims=True)
            spread = (widened - mean).reshape(block * levels, members).astype(BF16)
            first = jnp.dot(spread, weights_ref[0], preferred_element_type=F32)
            second = jnp.dot(spread, weights_ref[1], preferred_element_type=F32)
            tags = payload_ref[some, :, pl.ds(2 * members + half, META)].astype(F32)
            tags = tags.reshape(block * levels, META)[:, 2 + place : 3 + place]
            increment = jnp.where(tags == 2.0, second, first).reshape(block, levels, members)
            out_ref[some, :, lanes] = (mean + increment).astype(BF16)
            return carry

        lax.fori_loop(0, sources // block, apply, 0)


def exchange(x):
    return lax.all_to_all(x, AXES, split_axis=0, concat_axis=0, tiled=True)


VMEM = pl.BlockSpec(memory_space=pltpu.VMEM)
SMEM = pl.BlockSpec(memory_space=pltpu.SMEM)
HBM = pl.BlockSpec(memory_space=pltpu.HBM)


def on_device(background, col_target, obs_pert, innovation, obs_rinv, obs_loc, obs_patch):
    owners = lax.axis_size(AXES)
    cols, levels, members = background.shape
    obs = obs_pert.shape[0]
    width = 2 * members + members // 2 + META
    payload, col_slot = pl.pallas_call(
        pack_kernel,
        out_shape=(
            jax.ShapeDtypeStruct((owners, levels, width), BF16),
            jax.ShapeDtypeStruct((1, cols), jnp.int32),
        ),
        in_specs=[HBM] * 7,
        out_specs=(VMEM, HBM),
        scratch_shapes=[
            pltpu.VMEM(obs_pert.shape, BF16),
            pltpu.VMEM((1, obs), F32),
            pltpu.VMEM((1, obs), F32),
            pltpu.VMEM((2, obs), F32),
            pltpu.VMEM((2, obs), jnp.int32),
            pltpu.VMEM((1, cols), jnp.int32),
            pltpu.VMEM(background.shape, BF16),
            pltpu.VMEM((1, cols), jnp.int32),
            pltpu.SMEM((1, cols), jnp.int32),
            pltpu.SemaphoreType.DMA((9,)),
        ],
        name="pack",
    )(
        obs_pert,
        innovation[None, :],
        obs_rinv[None, :],
        obs_loc,
        obs_patch,
        col_target[None, :],
        background,
    )
    payload = exchange(payload)

    analysed = pl.pallas_call(
        analyse_kernel,
        out_shape=jax.ShapeDtypeStruct((owners, levels, CAP * members), BF16),
        in_specs=[VMEM],
        out_specs=VMEM,
        scratch_shapes=[pltpu.VMEM((PATCH_DEV, members, members), BF16)],
        compiler_params=pltpu.CompilerParams(vmem_limit_bytes=40 * MIB),
        name="analyse",
    )(payload)
    returned = exchange(analysed)

    return pl.pallas_call(
        unpack_kernel,
        out_shape=jax.ShapeDtypeStruct(background.shape, BF16),
        in_specs=[SMEM, VMEM],
        out_specs=HBM,
        scratch_shapes=[pltpu.VMEM(background.shape, BF16), pltpu.SemaphoreType.DMA((4,))],
        compiler_params=pltpu.CompilerParams(vmem_limit_bytes=16 * MIB),
        name="unpack",
    )(col_slot, returned)


def solution(mesh):
    return jax.shard_map(
        on_device,
        mesh=mesh,
        in_specs=(
            P(AXES, None, None),
            P(AXES),
            P(AXES, None),
            P(AXES),
            P(AXES),
            P(None, AXES),
            P(None, AXES),
        ),
        out_specs=P(AXES, None, None),
        check_vma=False,
    )
```

```python
import jax
import jax.numpy as jnp
from jax import lax
from jax.experimental import pallas as pl
from jax.experimental.pallas import tpu as pltpu
from jax.sharding import PartitionSpec as P

AXES = ("gx", "gy")
PATCH_DEV = 2
OCAP = 4
CAP = 2
LANES = 128
MIB = 1024 * 1024
F32 = jnp.float32
BF16 = jnp.bfloat16

GROUPS = 4
COL_ROWS = (0, 48)
OBS_ROWS = 32
META_ROWS = 80
BLOCK_ROWS = 82


def ranks(owner, owners):
    n = owner.shape[1]
    onehot = lax.broadcasted_iota(jnp.int32, (owners, n), 0) == owner
    earlier = lax.broadcasted_iota(jnp.int32, (n, n), 0) < lax.broadcasted_iota(jnp.int32, (n, n), 1)
    before = jnp.dot(
        jnp.where(onehot, 1.0, 0.0).astype(BF16),
        jnp.where(earlier, 1.0, 0.0).astype(BF16),
        preferred_element_type=F32,
    )
    rank = jnp.sum(jnp.where(onehot, before, 0.0), axis=0, keepdims=True)
    return rank.astype(jnp.int32)


def pack_kernel(
    pert_hbm, innov_hbm, rinv_hbm, loc_hbm, patch_hbm, target_hbm, cols_hbm, out_hbm, slot_hbm,
    pert_ref, innov_ref, rinv_ref, loc_ref, patch_ref, target_ref, held_cols, out_ref, slot_ref,
    order_ref, held_order, sems, out_sems,
):
    obs, members = pert_ref.shape
    owners = out_ref.shape[0]
    cols = held_cols.shape[0]
    block_ref = out_ref.reshape(owners, BLOCK_ROWS, LANES)
    pairs = (
        (target_hbm, target_ref), (patch_hbm, patch_ref), (rinv_hbm, rinv_ref), (loc_hbm, loc_ref),
        (innov_hbm, innov_ref), (pert_hbm, pert_ref), (cols_hbm, held_cols),
    )
    copies = [pltpu.make_async_copy(*pair, sems.at[i]) for i, pair in enumerate(pairs)]
    for copy in copies:
        copy.start()
    target_copy, *row_copies, cols_copy = copies
    target_copy.wait()

    target = target_ref[...]
    col_owner = target >> 1
    col_rank = ranks(col_owner, owners)
    slot_ref[...] = col_owner * CAP + col_rank
    slot_col = jnp.broadcast_to((col_owner * CAP + col_rank).astype(F32), (8, cols)).T[:, 0:1]
    places = lax.broadcasted_iota(jnp.int32, (cols, CAP * owners), 1).astype(F32)
    column = lax.broadcasted_iota(jnp.int32, (cols, CAP * owners), 0).astype(F32)
    order = jnp.sum(jnp.where(places == slot_col, column, 0.0), axis=0, keepdims=True)
    order_ref[...] = order.astype(jnp.int32)
    slot_copies = [
        pltpu.make_async_copy(order_ref, held_order, sems.at[7]),
        pltpu.make_async_copy(slot_ref, slot_hbm, sems.at[8]),
    ]
    for copy in slot_copies:
        copy.start()
    for copy in row_copies:
        copy.wait()

    patch = jnp.concatenate([patch_ref[0:1, :], patch_ref[1:2, :]], axis=1)
    owner = patch >> 1
    rank = ranks(owner, owners)
    root = jnp.sqrt(rinv_ref[...] * loc_ref[...])
    lifted = root * innov_ref[...]
    root = jnp.concatenate([root[0:1, :], root[1:2, :]], axis=1)
    lifted = jnp.concatenate([lifted[0:1, :], lifted[1:2, :]], axis=1)
    tag = ((patch & 1) + 1).astype(F32)
    col_tag = ((target & 1) + 1).astype(F32)
    rest = jnp.zeros((1, 2 * obs - cols), F32)
    col_lane = jnp.concatenate([(col_rank + 8).astype(F32), rest], axis=1)
    col_tag = jnp.concatenate([col_tag, rest], axis=1)
    nothing = jnp.zeros((2, 2 * obs), F32)
    by_entry = jnp.concatenate([root, lifted, tag, rank.astype(F32), col_lane, col_tag, nothing], axis=0).T

    pert = pert_ref[...].astype(F32)
    rows = (jnp.concatenate([pert, pert], axis=0) * by_entry[:, 0:1]).astype(BF16)
    lane = lax.broadcasted_iota(jnp.int32, (2 * obs, LANES), 1).astype(F32)
    meta = jnp.where(lane == by_entry[:, 3:4], by_entry[:, 1:2], 0.0)
    meta = jnp.where(lane == by_entry[:, 3:4] + OCAP, by_entry[:, 2:3], meta)
    lane = lax.broadcasted_iota(jnp.int32, (cols, LANES), 1).astype(F32)
    col_meta = jnp.where(lane == by_entry[:cols, 4:5], by_entry[:cols, 5:6], 0.0)

    place = lax.broadcasted_iota(jnp.int32, (8 * owners, 2 * obs), 0)
    chosen = jnp.where((place & ~OCAP) == owner * 8 + rank, 1.0, 0.0).astype(BF16)
    packed = jnp.dot(chosen, rows, preferred_element_type=F32)
    lower = (lax.broadcasted_iota(jnp.int32, (8 * owners, LANES), 0) & OCAP) == 0
    for pair in range(GROUPS // 2):
        first = 2 * pair * LANES
        both = jnp.where(lower, packed[:, first : first + LANES], packed[:, first + LANES : first + 2 * LANES])
        block_ref[:, OBS_ROWS + 8 * pair : OBS_ROWS + 8 * pair + 8, :] = both.reshape(owners, 8, LANES).astype(BF16)
    chosen = jnp.where((place >> 3) == owner, 1.0, 0.0).astype(BF16)
    place = lax.broadcasted_iota(jnp.int32, (8 * owners, cols), 0)
    col_chosen = jnp.where((place >> 3) == col_owner, 1.0, 0.0).astype(BF16)
    packed = jnp.dot(chosen, meta.astype(BF16), preferred_element_type=F32)
    packed += jnp.dot(col_chosen, col_meta.astype(BF16), preferred_element_type=F32)
    block_ref[:, META_ROWS:, :] = packed.reshape(owners, 8, LANES)[:, : BLOCK_ROWS - META_ROWS].astype(BF16)

    for copy in slot_copies:
        copy.wait()
    cols_copy.wait()

    chunks = out_sems.shape[0]
    block = owners // chunks
    copies = []
    for chunk in range(chunks):

        def put(i, carry):
            for place in range(CAP):
                column = held_cols[held_order[0, CAP * i + place]]
                for group in range(GROUPS):
                    first = COL_ROWS[place] + 8 * group
                    block_ref[i, first : first + 8, :] = column[:, group * LANES : (group + 1) * LANES]
            return carry

        lax.fori_loop(chunk * block, (chunk + 1) * block, put, 0, unroll=8)
        some = pl.ds(chunk * block, block)
        copies.append(pltpu.make_async_copy(out_ref.at[some], out_hbm.at[some], out_sems.at[chunk]))
        copies[-1].start()
    for copy in copies:
        copy.wait()


def unpack_kernel(slot_ref, cols_ref, out_hbm, held_cols, sems):
    cols, _, members = held_cols.shape
    chunks = sems.shape[0]
    block = cols // chunks
    copies = []
    for chunk in range(chunks):

        def take(i, carry):
            slot = slot_ref[0, i]
            lanes = pl.ds(pl.multiple_of((slot & 1) * members, members), members)
            held_cols[i] = cols_ref[slot >> 1, :, lanes]
            return carry

        lax.fori_loop(chunk * block, (chunk + 1) * block, take, 0, unroll=8)
        some = pl.ds(chunk * block, block)
        copies.append(pltpu.make_async_copy(held_cols.at[some], out_hbm.at[some], sems.at[chunk]))
        copies[-1].start()
    for copy in copies:
        copy.wait()


def product(a, b):
    return jnp.dot(a.astype(BF16), b.astype(BF16), preferred_element_type=F32)


def products(a, b):
    return [product(x, y) for x, y in zip(a, b)]


def two_steps(c, b):
    square = products(b, b)
    y = [2.25 + x * (-2.4375 + x * (1.6875 + x * (-0.5625 + x * 0.0625))) for x in c]
    first = [-2.4375 + x * (3.375 + x * (-1.6875 + x * 0.25)) for x in c]
    second = [1.6875 + x * (-1.6875 + x * 0.375) for x in c]
    third = [-0.5625 + x * 0.25 for x in c]
    inner = [0.0625 * s + t * x for s, t, x in zip(square, third, b)]
    high = products(inner, square)
    return y, [p + t * s + o * x for p, t, s, o, x in zip(high, second, square, first, b)]


def analyse_kernel(payload_ref, out_ref, weights_ref):
    sources, levels, _ = out_ref.shape
    members = weights_ref.shape[1]
    block_ref = payload_ref.reshape(sources, BLOCK_ROWS, LANES)
    meta = block_ref[:, META_ROWS:, :].astype(F32)[:, 0:1, :]
    meta = jnp.broadcast_to(meta, (sources, 8, LANES))
    col_tags = meta.reshape(sources * 8, LANES)

    half = sources // 2
    sublane = lax.broadcasted_iota(jnp.int32, (half, 8, LANES), 1)
    lane = lax.broadcasted_iota(jnp.int32, (half, 8, LANES), 2)

    def together(first):
        lower = block_ref[:half, first : first + 8, :].astype(F32)
        upper = block_ref[half:, first - OCAP : first - OCAP + 8, :].astype(F32)
        return jnp.where(sublane < OCAP, lower, upper).reshape(half * 8, LANES)

    row_meta = jnp.where(sublane < OCAP, meta[:half], meta[half:])
    row_meta = jnp.where((lane & (OCAP - 1)) == (sublane & (OCAP - 1)), row_meta, 0.0)
    row_meta = row_meta.reshape(half * 8, LANES)
    rows = jnp.concatenate([together(OBS_ROWS + OCAP * j) for j in range(GROUPS)] + [row_meta], axis=1)
    diagonal = lax.broadcasted_iota(jnp.int32, (members, members), 0) == lax.broadcasted_iota(
        jnp.int32, (members, members), 1
    )
    both = range(PATCH_DEV)
    flipped = rows.T
    tag = jnp.sum(flipped[members + OCAP : members + 2 * OCAP], axis=0, keepdims=True)
    rows = rows.astype(BF16)
    wide = [
        jnp.dot(
            jnp.where(tag == patch + 1, flipped[:members], 0.0).astype(BF16), rows, preferred_element_type=F32
        )
        for patch in both
    ]
    gram = [w[:, :members] for w in wide]
    largest = [jnp.sum(jnp.abs(g), axis=0, keepdims=True) for g in gram]
    bound = [(members - 1) + jnp.max(r, axis=1, keepdims=True) for r in largest]
    trace = [jnp.sum(jnp.where(diagonal, g, 0.0), axis=0, keepdims=True) for g in gram]
    trace = [jnp.sum(t, axis=1, keepdims=True) for t in trace]
    scale = [1.0 / v for v in bound]
    c = [(t / members + (members - 1)) * v for t, v in zip(trace, scale)]
    b = [g * v + jnp.where(diagonal, (members - 1) * v - s, 0.0) for g, v, s in zip(gram, scale, c)]
    z, d = two_steps(c, b)
    u = [2.0 * zi * di + p for zi, di, p in zip(z, d, products(d, d))]
    q = [p + zi * zi * bi + ci * ui for p, zi, bi, ci, ui in zip(products(u, b), z, b, c, u)]
    y, f = two_steps([zi * zi * ci for zi, ci in zip(z, c)], q)
    last = products(d, f)
    for patch in both:
        inverse = last[patch] + z[patch] * f[patch] + y[patch] * d[patch]
        inverse += jnp.where(diagonal, z[patch] * y[patch], 0.0)
        pull = jnp.sum(wide[patch][:, members : members + OCAP], axis=1, keepdims=True)
        once = jnp.sum(inverse * pull, axis=0, keepdims=True)
        mean_weight = jnp.sum(inverse * once, axis=1, keepdims=True) * scale[patch]
        root = jnp.sqrt((members - 1) * scale[patch])
        weights_ref[patch] = (root * inverse + mean_weight).astype(BF16)

    for place in range(CAP):
        groups = [
            block_ref[:, COL_ROWS[place] + 8 * j : COL_ROWS[place] + 8 * j + 8, :].astype(F32) for j in range(GROUPS)
        ]
        widened = jnp.concatenate(groups, axis=2)
        mean = jnp.mean(widened, axis=-1, keepdims=True)
        spread = (widened - mean).reshape(sources * levels, members).astype(BF16)
        first = jnp.dot(spread, weights_ref[0], preferred_element_type=F32)
        second = jnp.dot(spread, weights_ref[1], preferred_element_type=F32)
        increment = jnp.where(col_tags[:, 8 + place : 9 + place] == 2.0, second, first)
        increment = increment.reshape(sources, levels, members)
        out_ref[:, :, place * members : (place + 1) * members] = (mean + increment).astype(BF16)


def exchange(x):
    return lax.all_to_all(x, AXES, split_axis=0, concat_axis=0, tiled=True)


VMEM = pl.BlockSpec(memory_space=pltpu.VMEM)
SMEM = pl.BlockSpec(memory_space=pltpu.SMEM)
HBM = pl.BlockSpec(memory_space=pltpu.HBM)


def on_device(background, col_target, obs_pert, innovation, obs_rinv, obs_loc, obs_patch):
    owners = lax.axis_size(AXES)
    cols, levels, members = background.shape
    obs = obs_pert.shape[0]
    block = (owners, BLOCK_ROWS // 2, 2, LANES)
    payload, col_slot = pl.pallas_call(
        pack_kernel,
        out_shape=(
            jax.ShapeDtypeStruct(block, BF16),
            jax.ShapeDtypeStruct((1, cols), jnp.int32),
        ),
        in_specs=[HBM] * 7,
        out_specs=(HBM, HBM),
        scratch_shapes=[
            pltpu.VMEM(obs_pert.shape, BF16),
            pltpu.VMEM((1, obs), F32),
            pltpu.VMEM((1, obs), F32),
            pltpu.VMEM((2, obs), F32),
            pltpu.VMEM((2, obs), jnp.int32),
            pltpu.VMEM((1, cols), jnp.int32),
            pltpu.VMEM(background.shape, BF16),
            pltpu.VMEM(block, BF16),
            pltpu.VMEM((1, cols), jnp.int32),
            pltpu.VMEM((1, CAP * owners), jnp.int32),
            pltpu.SMEM((1, CAP * owners), jnp.int32),
            pltpu.SemaphoreType.DMA((9,)),
            pltpu.SemaphoreType.DMA((4,)),
        ],
        name="pack",
    )(
        obs_pert,
        innovation[None, :],
        obs_rinv[None, :],
        obs_loc,
        obs_patch,
        col_target[None, :],
        background,
    )
    payload = exchange(payload)

    analysed = pl.pallas_call(
        analyse_kernel,
        out_shape=jax.ShapeDtypeStruct((owners, levels, CAP * members), BF16),
        in_specs=[VMEM],
        out_specs=VMEM,
        scratch_shapes=[pltpu.VMEM((PATCH_DEV, members, members), BF16)],
        compiler_params=pltpu.CompilerParams(vmem_limit_bytes=40 * MIB),
        name="analyse",
    )(payload)
    returned = exchange(analysed)

    return pl.pallas_call(
        unpack_kernel,
        out_shape=jax.ShapeDtypeStruct(background.shape, BF16),
        in_specs=[SMEM, VMEM],
        out_specs=HBM,
        scratch_shapes=[pltpu.VMEM(background.shape, BF16), pltpu.SemaphoreType.DMA((4,))],
        compiler_params=pltpu.CompilerParams(vmem_limit_bytes=16 * MIB),
        name="unpack",
    )(col_slot, returned)


def solution(mesh):
    return jax.shard_map(
        on_device,
        mesh=mesh,
        in_specs=(
            P(AXES, None, None),
            P(AXES),
            P(AXES, None),
            P(AXES),
            P(AXES),
            P(None, AXES),
            P(None, AXES),
        ),
        out_specs=P(AXES, None, None),
        check_vma=False,
    )
```

```python
import jax
import jax.numpy as jnp
from jax import lax
from jax.experimental import pallas as pl
from jax.experimental.pallas import tpu as pltpu
from jax.sharding import PartitionSpec as P

AXES = ("gx", "gy")
PATCH_DEV = 2
OCAP = 4
CAP = 2
LANES = 128
MIB = 1024 * 1024
F32 = jnp.float32
BF16 = jnp.bfloat16

GROUPS = 4
COL_ROWS = (0, 48)
OBS_ROWS = 32
META_ROWS = 80
BLOCK_ROWS = 84


def ranks(owner, owners):
    n = owner.shape[1]
    onehot = lax.broadcasted_iota(jnp.int32, (owners, n), 0) == owner
    earlier = lax.broadcasted_iota(jnp.int32, (n, n), 0) < lax.broadcasted_iota(jnp.int32, (n, n), 1)
    before = jnp.dot(
        jnp.where(onehot, 1.0, 0.0).astype(BF16),
        jnp.where(earlier, 1.0, 0.0).astype(BF16),
        preferred_element_type=F32,
    )
    rank = jnp.sum(jnp.where(onehot, before, 0.0), axis=0, keepdims=True)
    return rank.astype(jnp.int32)


def pack_kernel(
    pert_hbm, innov_hbm, rinv_hbm, loc_hbm, patch_hbm, target_hbm, cols_hbm, out_hbm, slot_hbm,
    pert_ref, innov_ref, rinv_ref, loc_ref, patch_ref, target_ref, held_cols, out_ref, slot_ref,
    order_ref, held_order, sems, out_sems,
):
    obs, members = pert_ref.shape
    owners = out_ref.shape[0]
    cols = held_cols.shape[0]
    block_ref = out_ref.reshape(owners, BLOCK_ROWS, LANES)
    pairs = (
        (target_hbm, target_ref), (patch_hbm, patch_ref), (rinv_hbm, rinv_ref), (loc_hbm, loc_ref),
        (innov_hbm, innov_ref), (pert_hbm, pert_ref), (cols_hbm, held_cols),
    )
    copies = [pltpu.make_async_copy(*pair, sems.at[i]) for i, pair in enumerate(pairs)]
    for copy in copies:
        copy.start()
    target_copy, *row_copies, cols_copy = copies
    target_copy.wait()

    target = target_ref[...]
    col_owner = target >> 1
    col_rank = ranks(col_owner, owners)
    slot_ref[...] = col_owner * CAP + col_rank
    slot_col = jnp.broadcast_to((col_owner * CAP + col_rank).astype(F32), (8, cols)).T[:, 0:1]
    places = lax.broadcasted_iota(jnp.int32, (cols, CAP * owners), 1).astype(F32)
    column = lax.broadcasted_iota(jnp.int32, (cols, CAP * owners), 0).astype(F32)
    order = jnp.sum(jnp.where(places == slot_col, column, 0.0), axis=0, keepdims=True)
    order_ref[...] = order.astype(jnp.int32)
    slot_copies = [
        pltpu.make_async_copy(order_ref, held_order, sems.at[7]),
        pltpu.make_async_copy(slot_ref, slot_hbm, sems.at[8]),
    ]
    for copy in slot_copies:
        copy.start()
    for copy in row_copies:
        copy.wait()

    patch = jnp.concatenate([patch_ref[0:1, :], patch_ref[1:2, :]], axis=1)
    owner = patch >> 1
    rank = ranks(owner, owners)
    root = jnp.sqrt(rinv_ref[...] * loc_ref[...])
    lifted = root * innov_ref[...]
    root = jnp.concatenate([root[0:1, :], root[1:2, :]], axis=1)
    lifted = jnp.concatenate([lifted[0:1, :], lifted[1:2, :]], axis=1)
    tag = ((patch & 1) + 1).astype(F32)
    col_tag = ((target & 1) + 1).astype(F32)
    rest = jnp.zeros((1, 2 * obs - cols), F32)
    col_lane = jnp.concatenate([(col_rank + 8).astype(F32), rest], axis=1)
    col_tag = jnp.concatenate([col_tag, rest], axis=1)
    nothing = jnp.zeros((2, 2 * obs), F32)
    by_entry = jnp.concatenate([root, lifted, tag, rank.astype(F32), col_lane, col_tag, nothing], axis=0).T

    pert = pert_ref[...].astype(F32)
    rows = (jnp.concatenate([pert, pert], axis=0) * by_entry[:, 0:1]).astype(BF16)
    lane = lax.broadcasted_iota(jnp.int32, (2 * obs, LANES), 1).astype(F32)
    meta = jnp.where(lane == by_entry[:, 3:4], by_entry[:, 1:2], 0.0)
    meta = jnp.where(lane == by_entry[:, 3:4] + OCAP, by_entry[:, 2:3], meta)
    lane = lax.broadcasted_iota(jnp.int32, (cols, LANES), 1).astype(F32)
    col_meta = jnp.where(lane == by_entry[:cols, 4:5], by_entry[:cols, 5:6], 0.0)

    place = lax.broadcasted_iota(jnp.int32, (8 * owners, 2 * obs), 0)
    chosen = jnp.where((place & ~OCAP) == owner * 8 + rank, 1.0, 0.0).astype(BF16)
    packed = jnp.dot(chosen, rows, preferred_element_type=F32)
    lower = (lax.broadcasted_iota(jnp.int32, (8 * owners, LANES), 0) & OCAP) == 0
    for pair in range(GROUPS // 2):
        first = 2 * pair * LANES
        both = jnp.where(lower, packed[:, first : first + LANES], packed[:, first + LANES : first + 2 * LANES])
        block_ref[:, OBS_ROWS + 8 * pair : OBS_ROWS + 8 * pair + 8, :] = both.reshape(owners, 8, LANES).astype(BF16)
    chosen = jnp.where((place >> 3) == owner, 1.0, 0.0).astype(BF16)
    place = lax.broadcasted_iota(jnp.int32, (8 * owners, cols), 0)
    col_chosen = jnp.where((place >> 3) == col_owner, 1.0, 0.0).astype(BF16)
    packed = jnp.dot(chosen, meta.astype(BF16), preferred_element_type=F32)
    packed += jnp.dot(col_chosen, col_meta.astype(BF16), preferred_element_type=F32)
    block_ref[:, META_ROWS:, :] = packed.reshape(owners, 8, LANES)[:, : BLOCK_ROWS - META_ROWS].astype(BF16)

    for copy in slot_copies:
        copy.wait()
    cols_copy.wait()

    chunks = out_sems.shape[0]
    block = owners // chunks
    copies = []
    for chunk in range(chunks):

        def put(i, carry):
            for place in range(CAP):
                column = held_cols[held_order[0, CAP * i + place]].astype(F32)
                column = [column[:, j * LANES : (j + 1) * LANES] for j in range(GROUPS)]
                column = jnp.concatenate(column, axis=0).astype(BF16)
                block_ref[i, COL_ROWS[place] : COL_ROWS[place] + 8 * GROUPS, :] = column
            return carry

        lax.fori_loop(chunk * block, (chunk + 1) * block, put, 0, unroll=8)
        some = pl.ds(chunk * block, block)
        copies.append(pltpu.make_async_copy(out_ref.at[some], out_hbm.at[some], out_sems.at[chunk]))
        copies[-1].start()
    for copy in copies:
        copy.wait()


def unpack_kernel(slot_ref, cols_ref, out_hbm, held_cols, sems):
    cols, _, members = held_cols.shape
    chunks = sems.shape[0]
    block = cols // chunks
    copies = []
    for chunk in range(chunks):

        def take(i, carry):
            slot = slot_ref[0, i]
            lanes = pl.ds(pl.multiple_of((slot & 1) * members, members), members)
            held_cols[i] = cols_ref[slot >> 1, :, lanes]
            return carry

        lax.fori_loop(chunk * block, (chunk + 1) * block, take, 0, unroll=8)
        some = pl.ds(chunk * block, block)
        copies.append(pltpu.make_async_copy(held_cols.at[some], out_hbm.at[some], sems.at[chunk]))
        copies[-1].start()
    for copy in copies:
        copy.wait()


def product(a, b):
    return jnp.dot(a.astype(BF16), b.astype(BF16), preferred_element_type=F32)


def products(a, b):
    return [product(x, y) for x, y in zip(a, b)]


def two_steps(c, b):
    square = products(b, b)
    y = [2.25 + x * (-2.4375 + x * (1.6875 + x * (-0.5625 + x * 0.0625))) for x in c]
    first = [-2.4375 + x * (3.375 + x * (-1.6875 + x * 0.25)) for x in c]
    second = [1.6875 + x * (-1.6875 + x * 0.375) for x in c]
    third = [-0.5625 + x * 0.25 for x in c]
    inner = [0.0625 * s + t * x for s, t, x in zip(square, third, b)]
    high = products(inner, square)
    return y, [p + t * s + o * x for p, t, s, o, x in zip(high, second, square, first, b)]


def analyse_kernel(payload_ref, out_ref, weights_ref):
    sources, levels, _ = out_ref.shape
    members = weights_ref.shape[1]
    block_ref = payload_ref.reshape(sources, BLOCK_ROWS, LANES)
    meta = block_ref[:, META_ROWS:, :].astype(F32)[:, 0:1, :]
    meta = jnp.broadcast_to(meta, (sources, 8, LANES))
    col_tags = meta.reshape(sources * 8, LANES)

    half = sources // 2
    sublane = lax.broadcasted_iota(jnp.int32, (half, 8, LANES), 1)
    lane = lax.broadcasted_iota(jnp.int32, (half, 8, LANES), 2)

    lower = block_ref[:half, OBS_ROWS : OBS_ROWS + 16, :].astype(F32)
    lower_odd = block_ref[:half, OBS_ROWS + OCAP : OBS_ROWS + OCAP + 16, :].astype(F32)
    upper = block_ref[half:, OBS_ROWS : OBS_ROWS + 16, :].astype(F32)
    upper_odd = block_ref[half:, OBS_ROWS - OCAP : OBS_ROWS - OCAP + 16, :].astype(F32)

    def together(first):
        return jnp.where(
            sublane < OCAP,
            lower[:, first : first + 8] if first % 8 == 0 else lower_odd[:, first - OCAP : first + OCAP],
            upper_odd[:, first : first + 8] if first % 8 == 0 else upper[:, first - OCAP : first + OCAP],
        ).reshape(half * 8, LANES)

    row_meta = jnp.where(sublane < OCAP, meta[:half], meta[half:])
    row_meta = jnp.where((lane & (OCAP - 1)) == (sublane & (OCAP - 1)), row_meta, 0.0)
    row_meta = row_meta.reshape(half * 8, LANES)
    rows = jnp.concatenate([together(OCAP * j) for j in range(GROUPS)] + [row_meta], axis=1)
    diagonal = lax.broadcasted_iota(jnp.int32, (members, members), 0) == lax.broadcasted_iota(
        jnp.int32, (members, members), 1
    )
    both = range(PATCH_DEV)
    flipped = rows.T
    tag = jnp.sum(flipped[members + OCAP : members + 2 * OCAP], axis=0, keepdims=True)
    rows = rows.astype(BF16)
    wide = [
        jnp.dot(
            jnp.where(tag == patch + 1, flipped[:members], 0.0).astype(BF16), rows, preferred_element_type=F32
        )
        for patch in both
    ]
    gram = [w[:, :members] for w in wide]
    largest = [jnp.sum(jnp.abs(g), axis=0, keepdims=True) for g in gram]
    bound = [(members - 1) + jnp.max(r, axis=1, keepdims=True) for r in largest]
    trace = [jnp.sum(jnp.where(diagonal, g, 0.0), axis=0, keepdims=True) for g in gram]
    trace = [jnp.sum(t, axis=1, keepdims=True) for t in trace]
    scale = [1.0 / v for v in bound]
    c = [(t / members + (members - 1)) * v for t, v in zip(trace, scale)]
    b = [g * v + jnp.where(diagonal, (members - 1) * v - s, 0.0) for g, v, s in zip(gram, scale, c)]
    z, d = two_steps(c, b)
    u = [2.0 * zi * di + p for zi, di, p in zip(z, d, products(d, d))]
    q = [p + zi * zi * bi + ci * ui for p, zi, bi, ci, ui in zip(products(u, b), z, b, c, u)]
    y, f = two_steps([zi * zi * ci for zi, ci in zip(z, c)], q)
    last = products(d, f)
    for patch in both:
        inverse = last[patch] + z[patch] * f[patch] + y[patch] * d[patch]
        inverse += jnp.where(diagonal, z[patch] * y[patch], 0.0)
        pull = jnp.sum(wide[patch][:, members : members + OCAP], axis=1, keepdims=True)
        once = jnp.sum(inverse * pull, axis=0, keepdims=True)
        mean_weight = jnp.sum(inverse * once, axis=1, keepdims=True) * scale[patch]
        root = jnp.sqrt((members - 1) * scale[patch])
        weights_ref[patch] = (root * inverse + mean_weight).astype(BF16)

    for place in range(CAP):
        widened = block_ref[:, COL_ROWS[place] : COL_ROWS[place] + 8 * GROUPS, :].astype(F32)
        widened = jnp.concatenate([widened[:, 8 * j : 8 * j + 8, :] for j in range(GROUPS)], axis=2)
        mean = jnp.mean(widened, axis=-1, keepdims=True)
        spread = (widened - mean).reshape(sources * levels, members).astype(BF16)
        first = jnp.dot(spread, weights_ref[0], preferred_element_type=F32)
        second = jnp.dot(spread, weights_ref[1], preferred_element_type=F32)
        increment = jnp.where(col_tags[:, 8 + place : 9 + place] == 2.0, second, first)
        increment = increment.reshape(sources, levels, members)
        out_ref[:, :, place * members : (place + 1) * members] = (mean + increment).astype(BF16)


def exchange(x):
    return lax.all_to_all(x, AXES, split_axis=0, concat_axis=0, tiled=True)


VMEM = pl.BlockSpec(memory_space=pltpu.VMEM)
SMEM = pl.BlockSpec(memory_space=pltpu.SMEM)
HBM = pl.BlockSpec(memory_space=pltpu.HBM)


def on_device(background, col_target, obs_pert, innovation, obs_rinv, obs_loc, obs_patch):
    owners = lax.axis_size(AXES)
    cols, levels, members = background.shape
    obs = obs_pert.shape[0]
    block = (owners, BLOCK_ROWS // 4, 4, LANES)
    payload, col_slot = pl.pallas_call(
        pack_kernel,
        out_shape=(
            jax.ShapeDtypeStruct(block, BF16),
            jax.ShapeDtypeStruct((1, cols), jnp.int32),
        ),
        in_specs=[HBM] * 7,
        out_specs=(HBM, HBM),
        scratch_shapes=[
            pltpu.VMEM(obs_pert.shape, BF16),
            pltpu.VMEM((1, obs), F32),
            pltpu.VMEM((1, obs), F32),
            pltpu.VMEM((2, obs), F32),
            pltpu.VMEM((2, obs), jnp.int32),
            pltpu.VMEM((1, cols), jnp.int32),
            pltpu.VMEM(background.shape, BF16),
            pltpu.VMEM(block, BF16),
            pltpu.VMEM((1, cols), jnp.int32),
            pltpu.VMEM((1, CAP * owners), jnp.int32),
            pltpu.SMEM((1, CAP * owners), jnp.int32),
            pltpu.SemaphoreType.DMA((9,)),
            pltpu.SemaphoreType.DMA((4,)),
        ],
        name="pack",
    )(
        obs_pert,
        innovation[None, :],
        obs_rinv[None, :],
        obs_loc,
        obs_patch,
        col_target[None, :],
        background,
    )
    payload = exchange(payload)

    analysed = pl.pallas_call(
        analyse_kernel,
        out_shape=jax.ShapeDtypeStruct((owners, levels, CAP * members), BF16),
        in_specs=[VMEM],
        out_specs=VMEM,
        scratch_shapes=[pltpu.VMEM((PATCH_DEV, members, members), BF16)],
        compiler_params=pltpu.CompilerParams(vmem_limit_bytes=40 * MIB),
        name="analyse",
    )(payload)
    returned = exchange(analysed)

    return pl.pallas_call(
        unpack_kernel,
        out_shape=jax.ShapeDtypeStruct(background.shape, BF16),
        in_specs=[SMEM, VMEM],
        out_specs=HBM,
        scratch_shapes=[pltpu.VMEM(background.shape, BF16), pltpu.SemaphoreType.DMA((4,))],
        compiler_params=pltpu.CompilerParams(vmem_limit_bytes=16 * MIB),
        name="unpack",
    )(col_slot, returned)


def solution(mesh):
    return jax.shard_map(
        on_device,
        mesh=mesh,
        in_specs=(
            P(AXES, None, None),
            P(AXES),
            P(AXES, None),
            P(AXES),
            P(AXES),
            P(None, AXES),
            P(None, AXES),
        ),
        out_specs=P(AXES, None, None),
        check_vma=False,
    )
```

```python
import jax
import jax.numpy as jnp
from jax import lax
from jax.experimental import pallas as pl
from jax.experimental.pallas import tpu as pltpu
from jax.sharding import PartitionSpec as P

AXES = ("gx", "gy")
PATCH_DEV = 2
OCAP = 4
CAP = 2
LANES = 128
MIB = 1024 * 1024
F32 = jnp.float32
BF16 = jnp.bfloat16

GROUPS = 4
COL_ROWS = (0, 48)
OBS_ROWS = 32
META_ROWS = 80
BLOCK_ROWS = 84


def ranks(owner, owners):
    n = owner.shape[1]
    onehot = lax.broadcasted_iota(jnp.int32, (owners, n), 0) == owner
    earlier = lax.broadcasted_iota(jnp.int32, (n, n), 0) < lax.broadcasted_iota(jnp.int32, (n, n), 1)
    before = jnp.dot(
        jnp.where(onehot, 1.0, 0.0).astype(BF16),
        jnp.where(earlier, 1.0, 0.0).astype(BF16),
        preferred_element_type=F32,
    )
    rank = jnp.sum(jnp.where(onehot, before, 0.0), axis=0, keepdims=True)
    return rank.astype(jnp.int32)


def pack_kernel(
    pert_hbm, innov_hbm, rinv_hbm, loc_hbm, patch_hbm, target_hbm, cols_hbm, out_hbm, slot_hbm,
    pert_ref, innov_ref, rinv_ref, loc_ref, patch_ref, target_ref, held_cols, out_ref, slot_ref,
    order_ref, held_order, sems, out_sems,
):
    obs, members = pert_ref.shape
    owners = out_ref.shape[0]
    cols = held_cols.shape[0]
    block_ref = out_ref.reshape(owners, BLOCK_ROWS, LANES)
    pairs = (
        (target_hbm, target_ref), (patch_hbm, patch_ref), (rinv_hbm, rinv_ref), (loc_hbm, loc_ref),
        (innov_hbm, innov_ref), (pert_hbm, pert_ref), (cols_hbm, held_cols),
    )
    copies = [pltpu.make_async_copy(*pair, sems.at[i]) for i, pair in enumerate(pairs)]
    for copy in copies:
        copy.start()
    target_copy, *row_copies, cols_copy = copies
    target_copy.wait()

    target = target_ref[...]
    col_owner = target >> 1
    col_rank = ranks(col_owner, owners)
    slot_ref[...] = col_owner * CAP + col_rank
    slot_col = jnp.broadcast_to((col_owner * CAP + col_rank).astype(F32), (8, cols)).T[:, 0:1]
    places = lax.broadcasted_iota(jnp.int32, (cols, CAP * owners), 1).astype(F32)
    column = lax.broadcasted_iota(jnp.int32, (cols, CAP * owners), 0).astype(F32)
    order = jnp.sum(jnp.where(places == slot_col, column, 0.0), axis=0, keepdims=True)
    order_ref[...] = order.astype(jnp.int32)
    slot_copies = [
        pltpu.make_async_copy(order_ref, held_order, sems.at[7]),
        pltpu.make_async_copy(slot_ref, slot_hbm, sems.at[8]),
    ]
    for copy in slot_copies:
        copy.start()
    for copy in row_copies:
        copy.wait()

    patch = jnp.concatenate([patch_ref[0:1, :], patch_ref[1:2, :]], axis=1)
    owner = patch >> 1
    rank = ranks(owner, owners)
    root = jnp.sqrt(rinv_ref[...] * loc_ref[...])
    lifted = root * innov_ref[...]
    root = jnp.concatenate([root[0:1, :], root[1:2, :]], axis=1)
    lifted = jnp.concatenate([lifted[0:1, :], lifted[1:2, :]], axis=1)
    tag = ((patch & 1) + 1).astype(F32)
    col_tag = ((target & 1) + 1).astype(F32)
    rest = jnp.zeros((1, 2 * obs - cols), F32)
    col_lane = jnp.concatenate([(col_rank + 8).astype(F32), rest], axis=1)
    col_tag = jnp.concatenate([col_tag, rest], axis=1)
    nothing = jnp.zeros((2, 2 * obs), F32)
    by_entry = jnp.concatenate([root, lifted, tag, rank.astype(F32), col_lane, col_tag, nothing], axis=0).T

    pert = pert_ref[...].astype(F32)
    rows = (jnp.concatenate([pert, pert], axis=0) * by_entry[:, 0:1]).astype(BF16)
    lane = lax.broadcasted_iota(jnp.int32, (2 * obs, LANES), 1).astype(F32)
    meta = jnp.where(lane == by_entry[:, 3:4], by_entry[:, 1:2], 0.0)
    meta = jnp.where(lane == by_entry[:, 3:4] + OCAP, by_entry[:, 2:3], meta)
    lane = lax.broadcasted_iota(jnp.int32, (cols, LANES), 1).astype(F32)
    col_meta = jnp.where(lane == by_entry[:cols, 4:5], by_entry[:cols, 5:6], 0.0)

    place = lax.broadcasted_iota(jnp.int32, (8 * owners, 2 * obs), 0)
    chosen = jnp.where((place & ~OCAP) == owner * 8 + rank, 1.0, 0.0).astype(BF16)
    packed = jnp.dot(chosen, rows, preferred_element_type=F32)
    lower = (lax.broadcasted_iota(jnp.int32, (8 * owners, LANES), 0) & OCAP) == 0
    for pair in range(GROUPS // 2):
        first = 2 * pair * LANES
        both = jnp.where(lower, packed[:, first : first + LANES], packed[:, first + LANES : first + 2 * LANES])
        block_ref[:, OBS_ROWS + 8 * pair : OBS_ROWS + 8 * pair + 8, :] = both.reshape(owners, 8, LANES).astype(BF16)
    chosen = jnp.where((place >> 3) == owner, 1.0, 0.0).astype(BF16)
    place = lax.broadcasted_iota(jnp.int32, (8 * owners, cols), 0)
    col_chosen = jnp.where((place >> 3) == col_owner, 1.0, 0.0).astype(BF16)
    packed = jnp.dot(chosen, meta.astype(BF16), preferred_element_type=F32)
    packed += jnp.dot(col_chosen, col_meta.astype(BF16), preferred_element_type=F32)
    block_ref[:, META_ROWS:, :] = packed.reshape(owners, 8, LANES)[:, : BLOCK_ROWS - META_ROWS].astype(BF16)

    for copy in slot_copies:
        copy.wait()
    cols_copy.wait()

    chunks = out_sems.shape[0]
    block = owners // chunks
    copies = []
    for chunk in range(chunks):

        def put(i, carry):
            for place in range(CAP):
                column = held_cols[held_order[0, CAP * i + place]].astype(F32)
                column = [column[:, j * LANES : (j + 1) * LANES] for j in range(GROUPS)]
                column = jnp.concatenate(column, axis=0).astype(BF16)
                block_ref[i, COL_ROWS[place] : COL_ROWS[place] + 8 * GROUPS, :] = column
            return carry

        lax.fori_loop(chunk * block, (chunk + 1) * block, put, 0, unroll=8)
        some = pl.ds(chunk * block, block)
        copies.append(pltpu.make_async_copy(out_ref.at[some], out_hbm.at[some], out_sems.at[chunk]))
        copies[-1].start()
    for copy in copies:
        copy.wait()


def unpack_kernel(slot_ref, cols_ref, out_hbm, held_cols, sems):
    cols, _, members = held_cols.shape
    chunks = sems.shape[0]
    block = cols // chunks
    copies = []
    for chunk in range(chunks):

        def take(i, carry):
            slot = slot_ref[0, i]
            lanes = pl.ds(pl.multiple_of((slot & 1) * members, members), members)
            held_cols[i] = cols_ref[slot >> 1, :, lanes]
            return carry

        lax.fori_loop(chunk * block, (chunk + 1) * block, take, 0, unroll=8)
        some = pl.ds(chunk * block, block)
        copies.append(pltpu.make_async_copy(held_cols.at[some], out_hbm.at[some], sems.at[chunk]))
        copies[-1].start()
    for copy in copies:
        copy.wait()


def product(a, b):
    a, b = a.astype(BF16), b.astype(BF16)
    half = a.shape[0] // 2
    top = jnp.dot(a[:half], b, preferred_element_type=F32)
    last = jnp.dot(a[half:], b[:, half:], preferred_element_type=F32)
    return jnp.concatenate([top, jnp.concatenate([top[:, half:].T, last], axis=1)], axis=0)


def products(a, b):
    return [product(x, y) for x, y in zip(a, b)]


def two_steps(c, b):
    square = products(b, b)
    y = [2.25 + x * (-2.4375 + x * (1.6875 + x * (-0.5625 + x * 0.0625))) for x in c]
    first = [-2.4375 + x * (3.375 + x * (-1.6875 + x * 0.25)) for x in c]
    second = [1.6875 + x * (-1.6875 + x * 0.375) for x in c]
    third = [-0.5625 + x * 0.25 for x in c]
    inner = [0.0625 * s + t * x for s, t, x in zip(square, third, b)]
    high = products(inner, square)
    return y, [p + t * s + o * x for p, t, s, o, x in zip(high, second, square, first, b)]


def analyse_kernel(payload_ref, out_ref, weights_ref):
    sources, levels, _ = out_ref.shape
    members = weights_ref.shape[1]
    block_ref = payload_ref.reshape(sources, BLOCK_ROWS, LANES)
    meta = block_ref[:, META_ROWS:, :].astype(F32)[:, 0:1, :]
    meta = jnp.broadcast_to(meta, (sources, 8, LANES))
    col_tags = meta.reshape(sources * 8, LANES)

    half = sources // 2
    sublane = lax.broadcasted_iota(jnp.int32, (half, 8, LANES), 1)
    lane = lax.broadcasted_iota(jnp.int32, (half, 8, LANES), 2)

    lower = block_ref[:half, OBS_ROWS : OBS_ROWS + 16, :].astype(F32)
    lower_odd = block_ref[:half, OBS_ROWS + OCAP : OBS_ROWS + OCAP + 16, :].astype(F32)
    upper = block_ref[half:, OBS_ROWS : OBS_ROWS + 16, :].astype(F32)
    upper_odd = block_ref[half:, OBS_ROWS - OCAP : OBS_ROWS - OCAP + 16, :].astype(F32)

    def together(first):
        return jnp.where(
            sublane < OCAP,
            lower[:, first : first + 8] if first % 8 == 0 else lower_odd[:, first - OCAP : first + OCAP],
            upper_odd[:, first : first + 8] if first % 8 == 0 else upper[:, first - OCAP : first + OCAP],
        ).reshape(half * 8, LANES)

    row_meta = jnp.where(sublane < OCAP, meta[:half], meta[half:])
    row_meta = jnp.where((lane & (OCAP - 1)) == (sublane & (OCAP - 1)), row_meta, 0.0)
    row_meta = row_meta.reshape(half * 8, LANES)
    rows = jnp.concatenate([together(OCAP * j) for j in range(GROUPS)] + [row_meta], axis=1)
    diagonal = lax.broadcasted_iota(jnp.int32, (members, members), 0) == lax.broadcasted_iota(
        jnp.int32, (members, members), 1
    )
    both = range(PATCH_DEV)
    flipped = rows.T
    tag = jnp.sum(flipped[members + OCAP : members + 2 * OCAP], axis=0, keepdims=True)
    rows = rows.astype(BF16)
    wide = [
        jnp.dot(
            jnp.where(tag == patch + 1, flipped[:members], 0.0).astype(BF16), rows, preferred_element_type=F32
        )
        for patch in both
    ]
    gram = [w[:, :members] for w in wide]
    largest = [jnp.sum(jnp.abs(g), axis=0, keepdims=True) for g in gram]
    bound = [(members - 1) + jnp.max(r, axis=1, keepdims=True) for r in largest]
    trace = [jnp.sum(jnp.where(diagonal, g, 0.0), axis=0, keepdims=True) for g in gram]
    trace = [jnp.sum(t, axis=1, keepdims=True) for t in trace]
    scale = [1.0 / v for v in bound]
    c = [(t / members + (members - 1)) * v for t, v in zip(trace, scale)]
    b = [g * v + jnp.where(diagonal, (members - 1) * v - s, 0.0) for g, v, s in zip(gram, scale, c)]
    z, d = two_steps(c, b)
    u = [2.0 * zi * di + p for zi, di, p in zip(z, d, products(d, d))]
    q = [p + zi * zi * bi + ci * ui for p, zi, bi, ci, ui in zip(products(u, b), z, b, c, u)]
    y, f = two_steps([zi * zi * ci for zi, ci in zip(z, c)], q)
    last = products(d, f)
    for patch in both:
        inverse = last[patch] + z[patch] * f[patch] + y[patch] * d[patch]
        inverse += jnp.where(diagonal, z[patch] * y[patch], 0.0)
        pull = jnp.sum(wide[patch][:, members : members + OCAP], axis=1, keepdims=True)
        once = jnp.sum(inverse * pull, axis=0, keepdims=True)
        mean_weight = jnp.sum(inverse * once, axis=1, keepdims=True) * scale[patch]
        root = jnp.sqrt((members - 1) * scale[patch])
        weights_ref[patch] = (root * inverse + mean_weight).astype(BF16)

    for place in range(CAP):
        widened = block_ref[:, COL_ROWS[place] : COL_ROWS[place] + 8 * GROUPS, :].astype(F32)
        widened = jnp.concatenate([widened[:, 8 * j : 8 * j + 8, :] for j in range(GROUPS)], axis=2)
        mean = jnp.mean(widened, axis=-1, keepdims=True)
        spread = (widened - mean).reshape(sources * levels, members).astype(BF16)
        first = jnp.dot(spread, weights_ref[0], preferred_element_type=F32)
        second = jnp.dot(spread, weights_ref[1], preferred_element_type=F32)
        increment = jnp.where(col_tags[:, 8 + place : 9 + place] == 2.0, second, first)
        increment = increment.reshape(sources, levels, members)
        out_ref[:, :, place * members : (place + 1) * members] = (mean + increment).astype(BF16)


def exchange(x):
    return lax.all_to_all(x, AXES, split_axis=0, concat_axis=0, tiled=True)


VMEM = pl.BlockSpec(memory_space=pltpu.VMEM)
SMEM = pl.BlockSpec(memory_space=pltpu.SMEM)
HBM = pl.BlockSpec(memory_space=pltpu.HBM)


def on_device(background, col_target, obs_pert, innovation, obs_rinv, obs_loc, obs_patch):
    owners = lax.axis_size(AXES)
    cols, levels, members = background.shape
    obs = obs_pert.shape[0]
    block = (owners, BLOCK_ROWS // 4, 4, LANES)
    payload, col_slot = pl.pallas_call(
        pack_kernel,
        out_shape=(
            jax.ShapeDtypeStruct(block, BF16),
            jax.ShapeDtypeStruct((1, cols), jnp.int32),
        ),
        in_specs=[HBM] * 7,
        out_specs=(HBM, HBM),
        scratch_shapes=[
            pltpu.VMEM(obs_pert.shape, BF16),
            pltpu.VMEM((1, obs), F32),
            pltpu.VMEM((1, obs), F32),
            pltpu.VMEM((2, obs), F32),
            pltpu.VMEM((2, obs), jnp.int32),
            pltpu.VMEM((1, cols), jnp.int32),
            pltpu.VMEM(background.shape, BF16),
            pltpu.VMEM(block, BF16),
            pltpu.VMEM((1, cols), jnp.int32),
            pltpu.VMEM((1, CAP * owners), jnp.int32),
            pltpu.SMEM((1, CAP * owners), jnp.int32),
            pltpu.SemaphoreType.DMA((9,)),
            pltpu.SemaphoreType.DMA((4,)),
        ],
        name="pack",
    )(
        obs_pert,
        innovation[None, :],
        obs_rinv[None, :],
        obs_loc,
        obs_patch,
        col_target[None, :],
        background,
    )
    payload = exchange(payload)

    analysed = pl.pallas_call(
        analyse_kernel,
        out_shape=jax.ShapeDtypeStruct((owners, levels, CAP * members), BF16),
        in_specs=[VMEM],
        out_specs=VMEM,
        scratch_shapes=[pltpu.VMEM((PATCH_DEV, members, members), BF16)],
        compiler_params=pltpu.CompilerParams(vmem_limit_bytes=40 * MIB),
        name="analyse",
    )(payload)
    returned = exchange(analysed)

    return pl.pallas_call(
        unpack_kernel,
        out_shape=jax.ShapeDtypeStruct(background.shape, BF16),
        in_specs=[SMEM, VMEM],
        out_specs=HBM,
        scratch_shapes=[pltpu.VMEM(background.shape, BF16), pltpu.SemaphoreType.DMA((4,))],
        compiler_params=pltpu.CompilerParams(vmem_limit_bytes=16 * MIB),
        name="unpack",
    )(col_slot, returned)


def solution(mesh):
    return jax.shard_map(
        on_device,
        mesh=mesh,
        in_specs=(
            P(AXES, None, None),
            P(AXES),
            P(AXES, None),
            P(AXES),
            P(AXES),
            P(None, AXES),
            P(None, AXES),
        ),
        out_specs=P(AXES, None, None),
        check_vma=False,
    )
```

```python
import jax
import jax.numpy as jnp
from jax import lax
from jax.experimental import pallas as pl
from jax.experimental.pallas import tpu as pltpu
from jax.sharding import PartitionSpec as P

AXES = ("gx", "gy")
PATCH_DEV = 2
OCAP = 4
CAP = 2
LANES = 128
MIB = 1024 * 1024
F32 = jnp.float32
BF16 = jnp.bfloat16

GROUPS = 4
COL_ROWS = (0, 48)
OBS_ROWS = 32
META_ROWS = 80
BLOCK_ROWS = 84


def ranks(owner, owners):
    n = owner.shape[1]
    onehot = lax.broadcasted_iota(jnp.int32, (owners, n), 0) == owner
    earlier = lax.broadcasted_iota(jnp.int32, (n, n), 0) < lax.broadcasted_iota(jnp.int32, (n, n), 1)
    before = jnp.dot(
        jnp.where(onehot, 1.0, 0.0).astype(BF16),
        jnp.where(earlier, 1.0, 0.0).astype(BF16),
        preferred_element_type=F32,
    )
    rank = jnp.sum(jnp.where(onehot, before, 0.0), axis=0, keepdims=True)
    return rank.astype(jnp.int32)


def pack_kernel(
    pert_hbm, innov_hbm, rinv_hbm, loc_hbm, patch_hbm, target_hbm, cols_hbm, out_hbm, slot_hbm,
    pert_ref, innov_ref, rinv_ref, loc_ref, patch_ref, target_ref, held_cols, out_ref, slot_ref,
    order_ref, held_order, sems, out_sems,
):
    obs, members = pert_ref.shape
    owners = out_ref.shape[0]
    cols = held_cols.shape[0]
    block_ref = out_ref.reshape(owners, BLOCK_ROWS, LANES)
    pairs = (
        (target_hbm, target_ref), (patch_hbm, patch_ref), (rinv_hbm, rinv_ref), (loc_hbm, loc_ref),
        (innov_hbm, innov_ref), (pert_hbm, pert_ref), (cols_hbm, held_cols),
    )
    copies = [pltpu.make_async_copy(*pair, sems.at[i]) for i, pair in enumerate(pairs)]
    for copy in copies:
        copy.start()
    target_copy, *row_copies, cols_copy = copies
    target_copy.wait()

    target = target_ref[...]
    col_owner = target >> 1
    col_rank = ranks(col_owner, owners)
    slot_ref[...] = col_owner * CAP + col_rank
    slot_col = jnp.broadcast_to((col_owner * CAP + col_rank).astype(F32), (8, cols)).T[:, 0:1]
    places = lax.broadcasted_iota(jnp.int32, (cols, CAP * owners), 1).astype(F32)
    column = lax.broadcasted_iota(jnp.int32, (cols, CAP * owners), 0).astype(F32)
    order = jnp.sum(jnp.where(places == slot_col, column, 0.0), axis=0, keepdims=True)
    order_ref[...] = order.astype(jnp.int32)
    slot_copies = [
        pltpu.make_async_copy(order_ref, held_order, sems.at[7]),
        pltpu.make_async_copy(slot_ref, slot_hbm, sems.at[8]),
    ]
    for copy in slot_copies:
        copy.start()
    for copy in row_copies:
        copy.wait()

    patch = jnp.concatenate([patch_ref[0:1, :], patch_ref[1:2, :]], axis=1)
    owner = patch >> 1
    rank = ranks(owner, owners)
    root = jnp.sqrt(rinv_ref[...] * loc_ref[...])
    lifted = root * innov_ref[...]
    root = jnp.concatenate([root[0:1, :], root[1:2, :]], axis=1)
    lifted = jnp.concatenate([lifted[0:1, :], lifted[1:2, :]], axis=1)
    tag = ((patch & 1) + 1).astype(F32)
    col_tag = ((target & 1) + 1).astype(F32)
    rest = jnp.zeros((1, 2 * obs - cols), F32)
    col_lane = jnp.concatenate([(col_rank + 8).astype(F32), rest], axis=1)
    col_tag = jnp.concatenate([col_tag, rest], axis=1)
    nothing = jnp.zeros((2, 2 * obs), F32)
    by_entry = jnp.concatenate([root, lifted, tag, rank.astype(F32), col_lane, col_tag, nothing], axis=0).T

    pert = pert_ref[...].astype(F32)
    rows = (jnp.concatenate([pert, pert], axis=0) * by_entry[:, 0:1]).astype(BF16)
    lane = lax.broadcasted_iota(jnp.int32, (2 * obs, LANES), 1).astype(F32)
    meta = jnp.where(lane == by_entry[:, 3:4], by_entry[:, 1:2], 0.0)
    meta = jnp.where(lane == by_entry[:, 3:4] + OCAP, by_entry[:, 2:3], meta)
    lane = lax.broadcasted_iota(jnp.int32, (cols, LANES), 1).astype(F32)
    col_meta = jnp.where(lane == by_entry[:cols, 4:5], by_entry[:cols, 5:6], 0.0)

    place = lax.broadcasted_iota(jnp.int32, (8 * owners, 2 * obs), 0)
    chosen = jnp.where((place & ~OCAP) == owner * 8 + rank, 1.0, 0.0).astype(BF16)
    packed = jnp.dot(chosen, rows, preferred_element_type=F32)
    lower = (lax.broadcasted_iota(jnp.int32, (8 * owners, LANES), 0) & OCAP) == 0
    for pair in range(GROUPS // 2):
        first = 2 * pair * LANES
        both = jnp.where(lower, packed[:, first : first + LANES], packed[:, first + LANES : first + 2 * LANES])
        block_ref[:, OBS_ROWS + 8 * pair : OBS_ROWS + 8 * pair + 8, :] = both.reshape(owners, 8, LANES).astype(BF16)
    chosen = jnp.where((place >> 3) == owner, 1.0, 0.0).astype(BF16)
    place = lax.broadcasted_iota(jnp.int32, (8 * owners, cols), 0)
    col_chosen = jnp.where((place >> 3) == col_owner, 1.0, 0.0).astype(BF16)
    packed = jnp.dot(chosen, meta.astype(BF16), preferred_element_type=F32)
    packed += jnp.dot(col_chosen, col_meta.astype(BF16), preferred_element_type=F32)
    block_ref[:, META_ROWS:, :] = packed.reshape(owners, 8, LANES)[:, : BLOCK_ROWS - META_ROWS].astype(BF16)

    for copy in slot_copies:
        copy.wait()
    cols_copy.wait()

    chunks = out_sems.shape[0]
    block = owners // chunks
    copies = []
    for chunk in range(chunks):

        def put(i, carry):
            for place in range(CAP):
                column = held_cols[held_order[0, CAP * i + place]].astype(F32)
                column = [column[:, j * LANES : (j + 1) * LANES] for j in range(GROUPS)]
                column = jnp.concatenate(column, axis=0).astype(BF16)
                block_ref[i, COL_ROWS[place] : COL_ROWS[place] + 8 * GROUPS, :] = column
            return carry

        lax.fori_loop(chunk * block, (chunk + 1) * block, put, 0, unroll=8)
        some = pl.ds(chunk * block, block)
        copies.append(pltpu.make_async_copy(out_ref.at[some], out_hbm.at[some], out_sems.at[chunk]))
        copies[-1].start()
    for copy in copies:
        copy.wait()


def unpack_kernel(slot_ref, cols_ref, out_hbm, held_cols, sems):
    cols, _, members = held_cols.shape
    chunks = sems.shape[0]
    block = cols // chunks
    copies = []
    for chunk in range(chunks):

        def take(i, carry):
            slot = slot_ref[0, i]
            lanes = pl.ds(pl.multiple_of((slot & 1) * members, members), members)
            held_cols[i] = cols_ref[slot >> 1, :, lanes]
            return carry

        lax.fori_loop(chunk * block, (chunk + 1) * block, take, 0, unroll=8)
        some = pl.ds(chunk * block, block)
        copies.append(pltpu.make_async_copy(held_cols.at[some], out_hbm.at[some], sems.at[chunk]))
        copies[-1].start()
    for copy in copies:
        copy.wait()


def product(a, b):
    a, b = a.astype(BF16), b.astype(BF16)
    half = a.shape[0] // 2
    top = jnp.dot(a[:half], b, preferred_element_type=F32)
    last = jnp.dot(a[half:], b[:, half:], preferred_element_type=F32)
    return jnp.concatenate([top, jnp.concatenate([top[:, half:].T, last], axis=1)], axis=0)


def products(a, b):
    return [product(x, y) for x, y in zip(a, b)]


def two_steps(c, b):
    square = products(b, b)
    y = [2.25 + x * (-2.4375 + x * (1.6875 + x * (-0.5625 + x * 0.0625))) for x in c]
    first = [-2.4375 + x * (3.375 + x * (-1.6875 + x * 0.25)) for x in c]
    second = [1.6875 + x * (-1.6875 + x * 0.375) for x in c]
    third = [-0.5625 + x * 0.25 for x in c]
    inner = [0.0625 * s + t * x for s, t, x in zip(square, third, b)]
    high = products(inner, square)
    return y, [p + t * s + o * x for p, t, s, o, x in zip(high, second, square, first, b)]


def analyse_kernel(payload_ref, out_ref, weights_ref):
    sources, levels, _ = out_ref.shape
    members = weights_ref.shape[1]
    block_ref = payload_ref.reshape(sources, BLOCK_ROWS, LANES)
    meta = block_ref[:, META_ROWS:, :].astype(F32)[:, 0:1, :]
    meta = jnp.broadcast_to(meta, (sources, 8, LANES))
    col_tags = meta.reshape(sources * 8, LANES)

    half = sources // 2
    sublane = lax.broadcasted_iota(jnp.int32, (half, 8, LANES), 1)
    lane = lax.broadcasted_iota(jnp.int32, (half, 8, LANES), 2)

    lower = block_ref[:half, OBS_ROWS : OBS_ROWS + 16, :].astype(F32)
    lower_odd = block_ref[:half, OBS_ROWS + OCAP : OBS_ROWS + OCAP + 16, :].astype(F32)
    upper = block_ref[half:, OBS_ROWS : OBS_ROWS + 16, :].astype(F32)
    upper_odd = block_ref[half:, OBS_ROWS - OCAP : OBS_ROWS - OCAP + 16, :].astype(F32)

    def together(first):
        return jnp.where(
            sublane < OCAP,
            lower[:, first : first + 8] if first % 8 == 0 else lower_odd[:, first - OCAP : first + OCAP],
            upper_odd[:, first : first + 8] if first % 8 == 0 else upper[:, first - OCAP : first + OCAP],
        ).reshape(half * 8, LANES)

    row_meta = jnp.where(sublane < OCAP, meta[:half], meta[half:])
    row_meta = jnp.where((lane & (OCAP - 1)) == (sublane & (OCAP - 1)), row_meta, 0.0)
    row_meta = row_meta.reshape(half * 8, LANES)
    rows = jnp.concatenate([together(OCAP * j) for j in range(GROUPS)], axis=1)
    lifted = jnp.sum(jnp.where(lane < OCAP, row_meta.reshape(half, 8, LANES), 0.0), axis=2, keepdims=True)
    lifted = jnp.broadcast_to(lifted, (half, 8, LANES)).reshape(half * 8, LANES)
    diagonal = lax.broadcasted_iota(jnp.int32, (members, members), 0) == lax.broadcasted_iota(
        jnp.int32, (members, members), 1
    )
    both = range(PATCH_DEV)
    flipped = rows.T
    tag = jnp.sum(row_meta.T[OCAP : 2 * OCAP], axis=0, keepdims=True)
    rows = jnp.concatenate([rows, lifted], axis=1).astype(BF16)
    wide = [
        jnp.dot(
            jnp.where(tag == patch + 1, flipped, 0.0).astype(BF16), rows, preferred_element_type=F32
        )
        for patch in both
    ]
    gram = [w[:, :members] for w in wide]
    largest = [jnp.sum(jnp.abs(g), axis=0, keepdims=True) for g in gram]
    bound = [(members - 1) + jnp.max(r, axis=1, keepdims=True) for r in largest]
    trace = [jnp.sum(jnp.where(diagonal, g, 0.0), axis=0, keepdims=True) for g in gram]
    trace = [jnp.sum(t, axis=1, keepdims=True) for t in trace]
    scale = [1.0 / v for v in bound]
    c = [(t / members + (members - 1)) * v for t, v in zip(trace, scale)]
    b = [g * v + jnp.where(diagonal, (members - 1) * v - s, 0.0) for g, v, s in zip(gram, scale, c)]
    z, d = two_steps(c, b)
    u = [2.0 * zi * di + p for zi, di, p in zip(z, d, products(d, d))]
    q = [p + zi * zi * bi + ci * ui for p, zi, bi, ci, ui in zip(products(u, b), z, b, c, u)]
    y, f = two_steps([zi * zi * ci for zi, ci in zip(z, c)], q)
    last = products(d, f)
    for patch in both:
        inverse = last[patch] + z[patch] * f[patch] + y[patch] * d[patch]
        inverse += jnp.where(diagonal, z[patch] * y[patch], 0.0)
        pull = jnp.concatenate([wide[patch][:, members:]] * GROUPS, axis=1)
        once = jnp.sum(inverse * pull, axis=0, keepdims=True)
        mean_weight = jnp.sum(inverse * once, axis=1, keepdims=True) * scale[patch]
        root = jnp.sqrt((members - 1) * scale[patch])
        weights_ref[patch] = (root * inverse + mean_weight).astype(BF16)

    for place in range(CAP):
        widened = block_ref[:, COL_ROWS[place] : COL_ROWS[place] + 8 * GROUPS, :].astype(F32)
        widened = jnp.concatenate([widened[:, 8 * j : 8 * j + 8, :] for j in range(GROUPS)], axis=2)
        mean = jnp.mean(widened, axis=-1, keepdims=True)
        spread = (widened - mean).reshape(sources * levels, members).astype(BF16)
        first = jnp.dot(spread, weights_ref[0], preferred_element_type=F32)
        second = jnp.dot(spread, weights_ref[1], preferred_element_type=F32)
        increment = jnp.where(col_tags[:, 8 + place : 9 + place] == 2.0, second, first)
        increment = increment.reshape(sources, levels, members)
        out_ref[:, :, place * members : (place + 1) * members] = (mean + increment).astype(BF16)


def exchange(x):
    return lax.all_to_all(x, AXES, split_axis=0, concat_axis=0, tiled=True)


VMEM = pl.BlockSpec(memory_space=pltpu.VMEM)
SMEM = pl.BlockSpec(memory_space=pltpu.SMEM)
HBM = pl.BlockSpec(memory_space=pltpu.HBM)


def on_device(background, col_target, obs_pert, innovation, obs_rinv, obs_loc, obs_patch):
    owners = lax.axis_size(AXES)
    cols, levels, members = background.shape
    obs = obs_pert.shape[0]
    block = (owners, BLOCK_ROWS // 4, 4, LANES)
    payload, col_slot = pl.pallas_call(
        pack_kernel,
        out_shape=(
            jax.ShapeDtypeStruct(block, BF16),
            jax.ShapeDtypeStruct((1, cols), jnp.int32),
        ),
        in_specs=[HBM] * 7,
        out_specs=(HBM, HBM),
        scratch_shapes=[
            pltpu.VMEM(obs_pert.shape, BF16),
            pltpu.VMEM((1, obs), F32),
            pltpu.VMEM((1, obs), F32),
            pltpu.VMEM((2, obs), F32),
            pltpu.VMEM((2, obs), jnp.int32),
            pltpu.VMEM((1, cols), jnp.int32),
            pltpu.VMEM(background.shape, BF16),
            pltpu.VMEM(block, BF16),
            pltpu.VMEM((1, cols), jnp.int32),
            pltpu.VMEM((1, CAP * owners), jnp.int32),
            pltpu.SMEM((1, CAP * owners), jnp.int32),
            pltpu.SemaphoreType.DMA((9,)),
            pltpu.SemaphoreType.DMA((4,)),
        ],
        name="pack",
    )(
        obs_pert,
        innovation[None, :],
        obs_rinv[None, :],
        obs_loc,
        obs_patch,
        col_target[None, :],
        background,
    )
    payload = exchange(payload)

    analysed = pl.pallas_call(
        analyse_kernel,
        out_shape=jax.ShapeDtypeStruct((owners, levels, CAP * members), BF16),
        in_specs=[VMEM],
        out_specs=VMEM,
        scratch_shapes=[pltpu.VMEM((PATCH_DEV, members, members), BF16)],
        compiler_params=pltpu.CompilerParams(vmem_limit_bytes=40 * MIB),
        name="analyse",
    )(payload)
    returned = exchange(analysed)

    return pl.pallas_call(
        unpack_kernel,
        out_shape=jax.ShapeDtypeStruct(background.shape, BF16),
        in_specs=[SMEM, VMEM],
        out_specs=HBM,
        scratch_shapes=[pltpu.VMEM(background.shape, BF16), pltpu.SemaphoreType.DMA((4,))],
        compiler_params=pltpu.CompilerParams(vmem_limit_bytes=16 * MIB),
        name="unpack",
    )(col_slot, returned)


def solution(mesh):
    return jax.shard_map(
        on_device,
        mesh=mesh,
        in_specs=(
            P(AXES, None, None),
            P(AXES),
            P(AXES, None),
            P(AXES),
            P(AXES),
            P(None, AXES),
            P(None, AXES),
        ),
        out_specs=P(AXES, None, None),
        check_vma=False,
    )
```
